256 devices in a mesh: rep: 4 (over y), task: 64 (over z, x, core).
Axes of the slice: x: 4, y: 4, z: 8, core: 2. Of those that a mesh axis runs over, the one named last changes fastest.
Arguments:
- amps: bfloat16 [512, 256, 256], P('task', None, 'rep'), may hold values from -6 to 6
- integrals: bfloat16 [64, 256, 256], P(None, 'rep'), may hold values from -0.125 to 0.125
- a_index: int32 [24576], P('task'), may hold values from 0 to 7
- b_index: int32 [24576], P('task'), may hold values from 0 to 63
- live: int32 [24576], P('task'), may hold values 0 or 1
- owner: int32 [3072, 1], P('task'), may hold values from 0 to 63; in each aligned block of 48 rows (0 to 47, 48 to 95, ...) at most 2 rows name the same one
- target: int32 [3072], P('task'), may hold values from 0 to 7
Outputs:
- result: float32 [512, 256, 256], P('task', 'rep')
The draws below stay inside these ranges and needn't reach their ends.
Inputs may be any that keep to these rules, and one draw needn't show every extreme that they name: Among the 48 slots of one index of task (aligned blocks of 48 rows) no owner is named more than 2 times, a bound that some block reaches.
All inputs are finite; a program needn't handle non-finite values. No bound on the sum of `live` on one device may be relied on, other than what follows from the above.
Results may differ from the reference program's by a relative error of at most 0.013.
Values may be sent and summed in bfloat16 or wider, within the bound.
No kernel may reach another device: no remote copies, remote signals or barrier semaphores. Data moves between devices by JAX's collectives and lax.ppermute only.
A program may use at most 128 MiB of HBM per device.

```python
import math
import jax
import jax.numpy as jnp
import numpy as np
from jax import lax

TILE = 256
A_DEV = 8
NB = 64
SLOT_DEV = 48
TPS = 8
OWN_DEV = 8
CAP = 2
TASKS_DEV = 384
TASKS = 24576
SLOTS = 3072
A_TILES = 512
N_REP = 4
N_TASK = 64


def plant(entries, key, smallest, largest):
    dims = entries.shape
    place = [jax.random.randint(jax.random.fold_in(key, axis), (), 0, dims[axis]) for axis in range(len(dims))]
    entries = entries.at[tuple(place)].set(smallest)
    longest = dims.index(max(dims))
    place[longest] = (place[longest] + 1) % dims[longest]
    return entries.at[tuple(place)].set(largest)


def steps_of(stream_key, dims, shards, least, top_value):
    level, own = 1.0, jax.random.fold_in(stream_key, 6)
    for position, blocks in shards:
        heights = jnp.exp(jax.random.uniform(jax.random.fold_in(own, position), (blocks,), jnp.float32, least / len(shards), top_value / len(shards)))
        level = level * jnp.repeat(heights, dims[position] // blocks).reshape([-1 if axis == position else 1 for axis in range(len(dims))])
    return level


def rank_table(number_of, slope):
    portions = [(1 << 20) // math.isqrt(grade ** slope) + 1 for grade in range(1, number_of + 1)]
    spread = 1 + sum(portions) // (1 << 30)
    return np.cumsum(np.array([max(1, weight // spread) for weight in portions]))


def skewed_ids(key, extent, count, slope):
    grid = rank_table(count, slope)
    ticket = jax.random.randint(jax.random.fold_in(key, 1), extent, 0, int(grid[count - 1]))
    standing = jnp.searchsorted(jnp.asarray(grid, jnp.int32), ticket, side="right")
    return jax.random.permutation(jax.random.fold_in(key, 2), count)[standing].astype(jnp.int32)


def shared_out(own_key, own, number, rows, count, top, limit, skew):
    sequence = jax.random.permutation(own_key, count)
    packed, ordinary = shares(count, rows * top, limit, skew, True), shares(count, rows * top, limit, skew, False)
    places = jnp.arange(count)

    def named(lengths, offset_by):
        used = int((lengths > 0).sum())
        fixed = max(1, used // 4)
        moved = fixed + (places - fixed + offset_by * (used - fixed)) % max(1, count - fixed)
        return jnp.zeros((count,), jnp.int32).at[sequence[jnp.where(places < fixed, places, moved)]].set(jnp.asarray(lengths, jnp.int32))

    lengths = jnp.where(number % 4 == 0, named(packed, number // 4), named(ordinary, number - number // 4 - 1))
    mixed = jax.random.permutation(jax.random.fold_in(own, 3), count)
    giver, receiver = mixed[0:count // 2 * 2:2], mixed[1:count // 2 * 2:2]
    room = jnp.minimum(lengths[giver] - 1, limit - lengths[receiver]) // 2
    room = jnp.where((giver == sequence[0]) | (receiver == sequence[0]) | (lengths[receiver] == 0), 0, jnp.maximum(room, 0))
    moved = jax.random.randint(jax.random.fold_in(own, 4), (count // 2,), 0, 1 << 20) % (room + 1)
    lengths = lengths.at[giver].add(-moved).at[receiver].add(moved)
    members = jnp.searchsorted(jnp.cumsum(lengths), jnp.arange(rows * top), side="right").astype(jnp.int32)
    table = members.reshape(top, rows).T
    table = table[jax.random.permutation(jax.random.fold_in(own, 1), rows)]
    offset_by = jax.random.randint(jax.random.fold_in(own, 2), (rows, 1), 0, top)
    return jnp.take_along_axis(table, (jnp.arange(top)[None, :] + offset_by) % top, axis=1)


def shares(amount, total, limit, lean, full):
    loads = [(1 << 20) // math.isqrt(rank ** lean) + 1 for rank in range(1, amount + 1)]
    largest = limit if full else min(limit, max(-(-total // amount), total * loads[0] // sum(loads)))
    least = 1 if total - largest >= amount - 1 else 0
    given, spare = [largest] + [least] * (amount - 1), total - largest - least * (amount - 1)
    while spare > 0:
        candidates = [i for i in range(1, amount) if given[i] < largest] or [i for i in range(1, amount) if given[i] < limit]
        pool, left = sum([loads[i] for i in candidates]), spare
        for i in candidates:
            addition = min(limit - given[i], max(1, left * loads[i] // pool), spare)
            given[i] = given[i] + addition
            spare = spare - addition
    return np.array(given)


def gaussian(stream_key, dims, scale, limit, split=(), kind=jnp.bfloat16):
    array = jax.random.normal(stream_key, dims, jnp.float32) * scale
    if len(split) > 0:
        array = steps_of(stream_key, dims, split, -0.22, 0.18) * array
    return jnp.clip(array, min=-limit, max=limit).astype(kind)


def setup_inputs(seed: int = 0) -> dict:
    arg_keys = jax.random.split(jax.random.key(seed), 8)
    amps = gaussian(arg_keys[0], (A_TILES, TILE, TILE), 1.0, 6.0, ((0, 64), (2, 4)))
    integrals = gaussian(arg_keys[1], (NB, TILE, TILE), (TILE * TPS) ** -0.5, 0.125, ((1, 4),))
    a_index = plant(jax.random.randint(arg_keys[2], (TASKS,), 0, A_DEV), jax.random.fold_in(arg_keys[2], 1), 0, A_DEV - 1).astype(jnp.int32)
    b_index = plant(skewed_ids(arg_keys[3], (TASKS,), NB, 2), jax.random.fold_in(arg_keys[3], 3), 0, NB - 1).astype(jnp.int32)
    live = plant((jax.random.randint(arg_keys[4], (TASKS,), 0, 4) < 3).astype(jnp.int32), jax.random.fold_in(arg_keys[4], 1), 0, 1)
    owner_keys = jax.random.split(jax.random.fold_in(arg_keys[5], 1), SLOTS // SLOT_DEV)
    owner_turns = jax.random.permutation(jax.random.fold_in(arg_keys[5], 3), SLOTS // SLOT_DEV)
    owner = jax.vmap(lambda own, number: shared_out(jax.random.fold_in(arg_keys[5], 2), own, number, SLOT_DEV, N_TASK, 1, CAP, 2))(owner_keys, owner_turns).reshape((SLOTS, 1))
    target = plant(jax.random.randint(arg_keys[6], (SLOTS,), 0, OWN_DEV), jax.random.fold_in(arg_keys[6], 1), 0, OWN_DEV - 1).astype(jnp.int32)
    return {"amps": amps, "integrals": integrals, "a_index": a_index, "b_index": b_index, "live": live, "owner": owner, "target": target}


def reference(amps, integrals, a_index, b_index, live, owner, target):
    tile = amps.shape[1]
    quarter = tile // N_REP

    def group_slots(group):
        start = (group * TASKS_DEV).astype(jnp.int32)
        first = lax.dynamic_slice_in_dim(a_index, start, TASKS_DEV) + (group * A_DEV).astype(jnp.int32)
        second = lax.dynamic_slice_in_dim(b_index, start, TASKS_DEV)
        masked = lax.dynamic_slice_in_dim(live, start, TASKS_DEV)
        left = amps[first].astype(jnp.float32).reshape(SLOT_DEV, TPS, tile, N_REP, quarter)
        right = jnp.where(masked[:, None, None] > 0, integrals[second], jnp.zeros((), integrals.dtype))
        right = right.astype(jnp.float32).reshape(SLOT_DEV, TPS, N_REP, quarter, tile)
        partial_value = jnp.einsum("stirk,strkj->srij", left, right, precision=lax.Precision.HIGHEST)
        partial_value = lax.optimization_barrier(partial_value.astype(jnp.bfloat16)).astype(jnp.float32)
        return jnp.sum(partial_value, axis=1).astype(jnp.bfloat16)

    values = lax.map(group_slots, jnp.arange(N_TASK, dtype=jnp.int32))
    values = values.reshape(SLOTS, tile, tile)
    placed = owner[:, 0] * OWN_DEV + target
    empty = jnp.zeros((OWN_DEV * N_TASK, tile, tile), jnp.float32)
    return empty.at[placed].add(values.astype(jnp.float32))
```

```python
import functools

import jax
import jax.numpy as jnp
from jax import lax
from jax.experimental import pallas as pl
from jax.experimental.pallas import tpu as pltpu
from jax.sharding import Mesh
from jax.sharding import PartitionSpec as P

N_REP, N_Z, N_X, N_CORE = 4, 8, 4, 2
N_SRC = N_Z * N_CORE
OWN_DEV = 8
CAP = 2
TPS = 8
NB = 64
FIELDS = 32
ENTRIES = N_X * CAP
BF16 = jnp.bfloat16
F32 = jnp.float32


def slot_table(a_index, b_index, live, owner, target):
    slots = owner.shape[0]
    own = owner[:, 0]
    order = jnp.arange(slots, dtype=jnp.int32)
    earlier = (own[:, None] == own[None, :]) & (order[None, :] < order[:, None])
    standing = jnp.sum(earlier.astype(jnp.int32), axis=1)
    z, x, core = own // (N_X * N_CORE), (own // N_CORE) % N_X, own % N_CORE
    position = (z * N_CORE + core) * ENTRIES + x * CAP + standing
    chosen = jnp.arange(N_SRC * ENTRIES, dtype=jnp.int32)[:, None] == position[None, :]
    right = jnp.where(live > 0, b_index + 1, 0).reshape(slots, TPS)
    fields = jnp.concatenate(
        [
            (target + 1)[:, None],
            a_index.reshape(slots, TPS),
            right,
            jnp.zeros((slots, FIELDS - 1 - 2 * TPS), jnp.int32),
        ],
        axis=1,
    )
    table = jnp.dot(chosen.astype(F32), fields.astype(F32), precision=lax.Precision.HIGHEST)
    return table.astype(jnp.int32).reshape(N_SRC, ENTRIES * FIELDS)


def spread_rows(left):
    packed = left.transpose(0, 2, 1).reshape(4, 128, 4, 64)
    return packed.transpose(2, 0, 3, 1)


def join_k_kernel(parts_ref, out_ref):
    for pair in range(4):
        pieces = [parts_ref[r, pair] for r in range(N_REP)]
        for side in range(2):
            out_ref[2 * pair + side] = jnp.concatenate(
                [p[:, 64 * side : 64 * side + 64] for p in pieces], axis=1
            )


def join_k(parts):
    return pl.pallas_call(
        join_k_kernel,
        out_shape=jax.ShapeDtypeStruct((8, 64, 256), BF16),
        in_specs=[pl.BlockSpec(memory_space=pltpu.VMEM)],
        out_specs=pl.BlockSpec(memory_space=pltpu.VMEM),
        name="join_k",
    )(parts)


def products_kernel(place_ref, table_ref, *refs):
    lefts = refs[:N_SRC]
    right_hbm = refs[N_SRC]
    outs = refs[N_SRC + 1 : N_SRC + 1 + N_X]
    left, right, total, left_sems, right_sem = refs[N_SRC + 1 + N_X :]
    copies = [
        pltpu.make_async_copy(lefts[i], left.at[i], left_sems.at[i]) for i in range(N_SRC)
    ]
    copies.append(pltpu.make_async_copy(right_hbm, right, right_sem))
    for copy in copies:
        copy.start()
    total[...] = jnp.zeros_like(total)
    for copy in copies:
        copy.wait()
    my_x = place_ref[N_SRC]

    def one_entry(entry, carry):
        base = entry * FIELDS
        label = table_ref[base]

        @pl.when(label > 0)
        def _():
            source = entry // ENTRIES
            ahead = lax.rem((entry // CAP) % N_X - my_x + N_X, N_X)
            block = place_ref[source]
            spot = ahead * OWN_DEV + label - 1
            acc = jnp.zeros((64, 256), F32)
            for t in range(TPS):
                a = table_ref[base + 1 + t]
                b = table_ref[base + 1 + TPS + t]
                lhs = left[block, a]
                lhs = jnp.where(b > 0, lhs, jnp.zeros_like(lhs))
                b = jnp.maximum(b - 1, 0)
                rhs = jnp.concatenate([right[r, b] for r in range(N_REP)], axis=0)
                acc += jnp.dot(lhs, rhs, preferred_element_type=F32)
            total[spot] += acc

        return carry

    lax.fori_loop(0, N_SRC * ENTRIES, one_entry, 0)
    for ahead in range(N_X):
        part = total[ahead * OWN_DEV : (ahead + 1) * OWN_DEV]
        outs[ahead][...] = part.astype(outs[ahead].dtype)


def products(place, table, lefts, right):
    anywhere = pl.BlockSpec(memory_space=pl.ANY)
    shape = (OWN_DEV, 64, 256)
    return pl.pallas_call(
        products_kernel,
        out_shape=[jax.ShapeDtypeStruct(shape, F32 if s == 0 else BF16) for s in range(N_X)],
        grid_spec=pltpu.PrefetchScalarGridSpec(
            num_scalar_prefetch=2,
            grid=(),
            in_specs=[anywhere] * (N_SRC + 1),
            out_specs=[pl.BlockSpec(memory_space=pltpu.VMEM)] * N_X,
            scratch_shapes=[
                pltpu.VMEM((N_SRC, 8, 64, 256), BF16),
                pltpu.VMEM((N_REP, NB, 64, 256), BF16),
                pltpu.VMEM((N_X * OWN_DEV, 64, 256), F32),
                pltpu.SemaphoreType.DMA((N_SRC,)),
                pltpu.SemaphoreType.DMA,
            ],
        ),
        compiler_params=pltpu.CompilerParams(vmem_limit_bytes=40 * 1024 * 1024),
        cost_estimate=pl.CostEstimate(
            flops=2 * 384 * 64 * 256 * 256, bytes_accessed=13 << 20, transcendentals=0
        ),
        name="products",
    )(place, table, *lefts, right)


def away(value):
    perm = []
    for z in range(N_Z):
        perm.append((z * 2, ((z + 1) % N_Z) * 2))
        perm.append((z * 2 + 1, ((z - 1) % N_Z) * 2 + 1))
    return lax.ppermute(value, ("z", "core"), perm)


def other_core(value):
    return lax.ppermute(value, "core", [(0, 1), (1, 0)])


def gather_blocks(mine):
    own, other = mine, other_core(mine)
    blocks = [own, other]
    for distance in range(1, 4):
        own, other = away(own), away(other)
        blocks += [own, other, other_core(own), other_core(other)]
    own = away(own)
    blocks += [own, other_core(own)]
    z, core = lax.axis_index("z"), lax.axis_index("core")
    source = jnp.arange(N_SRC, dtype=jnp.int32)
    ahead = (source // N_CORE - z + N_Z) % N_Z
    ahead = jnp.where(core == 0, (N_Z - ahead) % N_Z, ahead)
    same = source % N_CORE == core
    first = jnp.where(same, 0, 1)
    place = jnp.where(ahead < 4, 4 * ahead - 2 + first, 4 * (N_Z - ahead) + 1 - first)
    place = jnp.where(ahead == 0, first, place)
    place = jnp.where(ahead == 4, 14 + first, place)
    return blocks, place.astype(jnp.int32)


def body(amps, integrals, a_index, b_index, live, owner, target):
    core = lax.axis_index("core")
    half = lax.dynamic_slice_in_dim(integrals, core * (NB // 2), NB // 2, 0)
    right = lax.all_gather(half, ("rep", "core"), tiled=False).reshape(N_REP, NB, 64, 256)
    table = slot_table(a_index, b_index, live, owner, target)
    table = lax.all_to_all(table, ("z", "core"), split_axis=0, concat_axis=0, tiled=True)
    parts = lax.all_to_all(spread_rows(amps), "rep", split_axis=0, concat_axis=0, tiled=True)
    blocks, place = gather_blocks(join_k(parts))
    place = jnp.concatenate([place, lax.axis_index("x").astype(jnp.int32)[None]])
    sums = products(place, table.reshape(-1), blocks, right)
    total = sums[0]
    for ahead in range(1, N_X):
        perm = [(i, (i + ahead) % N_X) for i in range(N_X)]
        total = total + lax.ppermute(sums[ahead], "x", perm).astype(F32)
    return total


def solution(mesh):
    devices = mesh.devices.reshape(N_REP, N_Z, N_X, N_CORE)
    fine = Mesh(devices, ("rep", "z", "x", "core"))
    task = ("z", "x", "core")
    in_specs = (
        P(task, None, "rep"),
        P(None, "rep", None),
        P(task),
        P(task),
        P(task),
        P(task, None),
        P(task),
    )
    return jax.shard_map(
        body, mesh=fine, in_specs=in_specs, out_specs=P(task, "rep", None), check_vma=False
    )
```

```python
import jax
import jax.numpy as jnp
from jax import lax
from jax.experimental import pallas as pl
from jax.experimental.pallas import tpu as pltpu
from jax.sharding import Mesh
from jax.sharding import PartitionSpec as P

N_REP, N_Z, N_X, N_CORE = 4, 8, 4, 2
N_SRC = N_Z * N_CORE
A_DEV = 8
OWN_DEV = 8
TPS = 8
NB = 64
HALF = NB // 2
PART = HALF // 2
QUARTER = 64
TILE = 256
MOST = 128
LABELS = 2 * N_SRC
SPOTS = N_X * OWN_DEV
GROUP = 4
WIDE = 8
LIST = 2304
NOWHERE = 2 * SPOTS * 512
TRASH = LIST - 1
ROWS = A_DEV * QUARTER
BLOCK = ROWS + LABELS
VMEM_LIMIT = 56 * 1024 * 1024
BF16 = jnp.bfloat16
F32 = jnp.float32
I32 = jnp.int32
VMEM = pl.BlockSpec(memory_space=pltpu.VMEM)
SMEM = pl.BlockSpec(memory_space=pltpu.SMEM)
ANY = pl.BlockSpec(memory_space=pl.ANY)


def product_table(x, a_index, b_index, live, owner, target):
    products = a_index.shape[0]
    own = jnp.repeat(owner[:, 0], TPS)
    z, own_x, own_core = own // (N_X * N_CORE), (own // N_CORE) % N_X, own % N_CORE
    half = b_index // HALF
    place = jnp.where(live > 0, z * N_CORE + half, -1)
    away = (own_core != half).astype(I32) * SPOTS
    spot = away + ((own_x - x + N_X) % N_X) * OWN_DEV + jnp.repeat(target, TPS) + 1
    order = jnp.arange(products, dtype=I32)
    earlier = (place[:, None] == place[None, :]) & (order[None, :] < order[:, None])
    standing = jnp.sum(earlier.astype(I32), axis=1)
    alike = earlier & (b_index[:, None] == b_index[None, :])
    rank = jnp.sum(alike.astype(I32), axis=1)
    at = jnp.where(live > 0, place * MOST + standing, -1)
    chosen = jnp.arange(N_SRC * MOST, dtype=I32)[:, None] == at[None, :]
    fields = jnp.stack([spot, a_index, b_index % HALF, rank]).astype(BF16)
    table = jnp.dot(fields, chosen.astype(BF16).T, preferred_element_type=F32).astype(BF16)
    return table.reshape(2, 2, N_SRC, MOST).transpose(2, 0, 1, 3).reshape(LABELS, 2 * MOST)


def spread_kernel(rep_ref, left_ref, *refs):
    outs, turned = refs[:N_REP], refs[N_REP]
    for pair in range(4):
        tile = left_ref[2 * pair : 2 * pair + 2].reshape(2 * QUARTER, TILE)
        turned[pair] = tile.T
    for shift in range(N_REP):
        to = lax.rem(rep_ref[0] + shift, N_REP)
        first = pl.multiple_of(to * QUARTER, QUARTER)
        for pair in range(4):
            outs[shift][pair] = turned[pair, pl.ds(first, QUARTER), :]


def spread_rows(rep, left):
    return pl.pallas_call(
        spread_kernel,
        out_shape=[jax.ShapeDtypeStruct((4, QUARTER, 2 * QUARTER), BF16)] * N_REP,
        in_specs=[SMEM, VMEM],
        out_specs=[VMEM] * N_REP,
        scratch_shapes=[pltpu.VMEM((4, TILE, 2 * QUARTER), BF16)],
        name="spread_rows",
    )(rep, left.transpose(0, 2, 1))


def join_kernel(table_ref, *refs):
    parts, out_ref = refs[:N_REP], refs[N_REP]
    for pair in range(4):
        pieces = [part[pair] for part in parts]
        for side in range(2):
            first = (2 * pair + side) * QUARTER
            out_ref[first : first + QUARTER] = jnp.concatenate(
                [p[:, QUARTER * side : QUARTER * (side + 1)] for p in pieces], axis=1
            )
    out_ref[ROWS:BLOCK] = table_ref[...]


def join_k(table, parts):
    return pl.pallas_call(
        join_kernel,
        out_shape=jax.ShapeDtypeStruct((BLOCK, TILE), BF16),
        in_specs=[VMEM] * (N_REP + 1),
        out_specs=VMEM,
        name="join_k",
    )(table, *parts)


def sort_products(me, left, labels, lines, scalars, listed, sem):
    for block in range(N_SRC):
        labels[block] = left[block, ROWS:BLOCK].astype(F32)
    for block in range(N_SRC):
        first, second = labels[block, pl.ds(2 * me, 1), :], labels[block, pl.ds(2 * me + 1, 1), :]
        spot, a, b, rank = first[:, :MOST], first[:, MOST:], second[:, :MOST], second[:, MOST:]
        code = (spot - 1.0) * 512.0 + b * 8.0 + a + rank * 65536.0
        lines[block : block + 1, :] = jnp.where(spot > 0.0, code.astype(I32), HALF * 8)
    codes = lines[:N_SRC]
    tile = (codes >> 3) & 63
    lane = lax.broadcasted_iota(I32, (N_SRC, MOST), 1)
    sizes = jnp.zeros((N_SRC, MOST), F32)
    for b in range(HALF):
        size = jnp.sum((tile == b).astype(F32), axis=1, keepdims=True)
        sizes = jnp.where(lane == b, size, sizes)
    counts = jnp.sum(sizes, axis=1, keepdims=True)
    row = lax.broadcasted_iota(I32, (N_SRC, N_SRC), 0)
    column = lax.broadcasted_iota(I32, (N_SRC, N_SRC), 1)
    before = jnp.dot((column < row).astype(F32), sizes, precision=lax.Precision.HIGHEST)
    all_sizes = jnp.broadcast_to(jnp.sum(sizes, axis=0, keepdims=True), (8, MOST))
    groups = ((all_sizes.astype(I32) + GROUP - 1) // GROUP).astype(F32)
    row = lax.broadcasted_iota(I32, (MOST, MOST), 0)
    column = lax.broadcasted_iota(I32, (MOST, MOST), 1)
    starts = GROUP * jnp.dot(groups, (row < column).astype(F32), precision=lax.Precision.HIGHEST)
    base = jnp.where(lane < HALF, before + starts[:1], TRASH)
    lines[N_SRC : 2 * N_SRC] = base.astype(I32)
    lines[2 * N_SRC : 3 * N_SRC] = jnp.broadcast_to(counts, (N_SRC, MOST)).astype(I32)
    lines[3 * N_SRC : 3 * N_SRC + 8] = (starts + all_sizes).astype(I32)
    lines[3 * N_SRC + 8 : 3 * N_SRC + 16] = starts.astype(I32)
    copy = pltpu.make_async_copy(lines, scalars, sem)
    copy.start()
    copy.wait()
    total = scalars[3 * N_SRC + 8, HALF]
    for b in range(HALF):
        end = scalars[3 * N_SRC, b]
        for u in range(GROUP - 1):
            listed[end + u] = NOWHERE + b * 8
    for u in range(GROUP * WIDE):
        listed[total + u] = jnp.int32(NOWHERE)

    def one_source(block, carry):
        def some_products(i, carry):
            for u in range(8):
                code = scalars[block, i * 8 + u]
                to = scalars[N_SRC + block, (code >> 3) & 63] + (code >> 16)
                listed[to] = (code & 65535) + (block << 16)
            return carry

        return lax.fori_loop(0, (scalars[2 * N_SRC + block, 0] + 7) // 8, some_products, carry)

    lax.fori_loop(0, N_SRC, one_source, 0)
    return total


RIGHT_PLACES = [(quarter, first) for quarter in (0, 1, 3, 2) for first in (0, PART)]
N_RIGHT = len(RIGHT_PLACES)


def products_kernel(me_ref, *refs):
    lefts, rights, refs = refs[:N_SRC], refs[N_SRC : N_SRC + N_RIGHT], refs[N_SRC + N_RIGHT :]
    away_ref, home_ref, left, right, total, labels, lines, scalars, listed = refs[:9]
    left_sems, right_sems, lines_sem = refs[9:]
    copies = [
        pltpu.make_async_copy(lefts[i], left.at[i], left_sems.at[i]) for i in range(N_SRC)
    ]
    fetches = [
        pltpu.make_async_copy(rights[i], right.at[q, pl.ds(b, PART)], right_sems.at[i])
        for i, (q, b) in enumerate(RIGHT_PLACES)
    ]
    for copy in copies + fetches:
        copy.start()
    total[...] = jnp.zeros_like(total)
    for copy in copies:
        copy.wait()
    length = sort_products(me_ref[0], left, labels, lines, scalars, listed, lines_sem)
    for fetch in fetches:
        fetch.wait()

    def step(i, carry):
        sums = []
        for w in range(WIDE):
            spots, rows = [], []
            for u in range(GROUP):
                code = listed[(i * WIDE + w) * GROUP + u]
                first = pl.multiple_of((code & 7) * QUARTER, QUARTER)
                rows.append(left[code >> 16, pl.ds(first, QUARTER), :])
                spots.append((code >> 9) & 127)
                b = (code >> 3) & (HALF - 1)
            tile = jnp.concatenate([right[q, b] for q in range(N_REP)], axis=0)
            lhs = jnp.concatenate(rows, axis=0)
            sums.append((spots, jnp.dot(lhs, tile, preferred_element_type=F32)))
        for spots, value in sums:
            for u in range(GROUP):
                total[spots[u]] += value[u * QUARTER : (u + 1) * QUARTER]
        return carry

    lax.fori_loop(0, (length + GROUP * WIDE - 1) // (GROUP * WIDE), step, 0)
    home_ref[...] = total[:SPOTS].astype(BF16)
    away_ref[...] = total[SPOTS : 2 * SPOTS].astype(BF16)


def products(me, lefts, rights):
    shape = (SPOTS, QUARTER, TILE)
    return pl.pallas_call(
        products_kernel,
        out_shape=[jax.ShapeDtypeStruct(shape, BF16)] * 2,
        in_specs=[SMEM] + [ANY] * (N_SRC + N_RIGHT),
        out_specs=[VMEM] * 2,
        scratch_shapes=[
            pltpu.VMEM((N_SRC, BLOCK, TILE), BF16),
            pltpu.VMEM((N_REP, HALF, QUARTER, TILE), BF16),
            pltpu.VMEM((2 * SPOTS + 1, QUARTER, TILE), F32),
            pltpu.VMEM((N_SRC, LABELS, TILE), F32),
            pltpu.VMEM((4 * N_SRC, MOST), I32),
            pltpu.SMEM((4 * N_SRC, MOST), I32),
            pltpu.SMEM((LIST,), I32),
            pltpu.SemaphoreType.DMA((N_SRC,)),
            pltpu.SemaphoreType.DMA((N_RIGHT,)),
            pltpu.SemaphoreType.DMA,
        ],
        compiler_params=pltpu.CompilerParams(vmem_limit_bytes=VMEM_LIMIT),
        cost_estimate=pl.CostEstimate(
            flops=2 * 384 * 64 * 256 * 256, bytes_accessed=10 << 20, transcendentals=0
        ),
        name="products",
    )(me, *lefts, *rights)


def shift_by(value, axis, size, step):
    return lax.ppermute(value, axis, [(i, (i + step) % size) for i in range(size)])


def apart(value):
    perm = []
    for i in range(N_Z):
        perm.append((i * 2, ((i + 1) % N_Z) * 2))
        perm.append((i * 2 + 1, ((i - 1) % N_Z) * 2 + 1))
    return lax.ppermute(value, ("z", "core"), perm)


def other_core(value):
    return lax.ppermute(value, "core", [(0, 1), (1, 0)])


def gather(mine, first, second):
    back_first, ahead_second = shift_by(first, "rep", N_REP, 1), shift_by(second, "rep", N_REP, -1)
    back_second, ahead_first = shift_by(second, "rep", N_REP, 1), shift_by(first, "rep", N_REP, -1)
    own, other = mine, other_core(mine)
    blocks = [own, other]
    for distance in range(1, 4):
        if distance == 3:
            own, other, back_first, ahead_second = lax.optimization_barrier(
                (own, other, back_first, ahead_second)
            )
        own, other = apart(own), apart(other)
        blocks += [own, other, other_core(own), other_core(other)]
    own = apart(own)
    far_first = shift_by(back_first, "rep", N_REP, 1)
    far_second = shift_by(ahead_second, "rep", N_REP, -1)
    rights = [
        first, second, back_first, back_second, ahead_first, ahead_second, far_first, far_second
    ]
    return blocks + [own, other_core(own)], rights


def body(amps, integrals, a_index, b_index, live, owner, target):
    rep, z, x, core = [lax.axis_index(n).astype(I32) for n in ("rep", "z", "x", "core")]
    pieces = spread_rows(rep[None], amps)
    first = lax.dynamic_slice_in_dim(integrals, core * HALF, PART, 0)
    second = lax.dynamic_slice_in_dim(integrals, core * HALF + PART, PART, 0)
    table = product_table(x, a_index, b_index, live, owner, target)
    parts = [pieces[0]] + [shift_by(pieces[s], "rep", N_REP, s) for s in range(1, N_REP)]
    first, second, *parts = lax.optimization_barrier((first, second, *parts))
    lefts, rights = gather(join_k(table, parts), first, second)
    away, home = products((z * N_CORE + core)[None], lefts, rights)
    sums = home.astype(F32) + other_core(away).astype(F32)
    sums = sums.reshape(N_X, OWN_DEV, QUARTER, TILE)
    total = sums[0]
    for step in range(1, N_X):
        total = total + shift_by(sums[step].astype(BF16), "x", N_X, step).astype(F32)
    return total


def solution(mesh):
    devices = mesh.devices.reshape(N_REP, N_Z, N_X, N_CORE)
    fine = Mesh(devices, ("rep", "z", "x", "core"))
    task = ("z", "x", "core")
    in_specs = (
        P(task, None, "rep"),
        P(None, "rep", None),
        P(task),
        P(task),
        P(task),
        P(task, None),
        P(task),
    )
    return jax.shard_map(
        body, mesh=fine, in_specs=in_specs, out_specs=P(task, "rep", None), check_vma=False
    )
```

```python
import jax
import jax.numpy as jnp
from jax import lax
from jax.experimental import pallas as pl
from jax.experimental.pallas import tpu as pltpu
from jax.sharding import Mesh
from jax.sharding import PartitionSpec as P

N_REP, N_Z, N_X, N_CORE = 4, 8, 4, 2
N_SRC = N_Z
A_DEV = 8
OWN_DEV = 8
TPS = 8
NB = 64
HALF = NB // 2
QUARTER = 64
TILE = 256
MOST = 128
LABELS = 2 * N_Z
SPOTS = N_X * OWN_DEV
GROUP = 4
WIDE = 8
LIST = 1280
NOWHERE = 2.0 * SPOTS * 4096
SORT_COST = 10**10
ROWS = A_DEV * QUARTER
BLOCK = ROWS + LABELS
TABLE_COST = 4 * 10**9
VMEM_LIMIT = 56 * 1024 * 1024
BF16 = jnp.bfloat16
F32 = jnp.float32
I32 = jnp.int32
VMEM = pl.BlockSpec(memory_space=pltpu.VMEM)
SMEM = pl.BlockSpec(memory_space=pltpu.SMEM)
ANY = pl.BlockSpec(memory_space=pl.ANY)


def table_kernel(x_ref, a_ref, b_ref, live_ref, owner_ref, target_ref, out_ref, lines):
    products, slots = a_ref.shape[0], owner_ref.shape[0]
    x = x_ref[0]
    row = lax.broadcasted_iota(I32, (8, slots), 0)
    named = jnp.where(row == 0, owner_ref[...][None], jnp.where(row == 1, target_ref[...][None], 0))
    slot = lax.broadcasted_iota(I32, (slots, products), 0)
    spread = lax.broadcasted_iota(I32, (slots, products), 1) // TPS == slot
    named = jnp.dot(named.astype(F32), spread.astype(F32), precision=lax.Precision.HIGHEST)
    own, target = named[0:1].astype(I32), named[1:2].astype(I32)
    a, b = a_ref[...][None], b_ref[...][None]
    place = jnp.where(live_ref[...][None] > 0, own // (N_X * N_CORE), -1)
    spot = own % N_CORE * SPOTS + ((own // N_CORE - x) & (N_X - 1)) * OWN_DEV + target + 1
    row = lax.broadcasted_iota(I32, (8, products), 0)
    turned = jnp.where(row == 0, place, b).astype(F32).T
    same = turned[:, 0:1] == place.astype(F32)
    order = lax.broadcasted_iota(I32, (products, products), 0)
    same = same & (order < lax.broadcasted_iota(I32, (products, products), 1))
    alike = same & (turned[:, 1:2] == b.astype(F32))
    standing = jnp.sum(same.astype(F32), axis=0, keepdims=True).astype(I32)
    rank = jnp.sum(alike.astype(F32), axis=0, keepdims=True).astype(I32)
    at = jnp.where(place >= 0, place * MOST + standing, -1)
    fields = jnp.where(row == 0, spot, jnp.where(row == 1, a, jnp.where(row == 2, b, rank)))
    fields = fields.astype(F32).astype(BF16)
    position = lax.broadcasted_iota(I32, (MOST, products), 0)
    for place in range(N_Z):
        chosen = (at == position + place * MOST).astype(F32).astype(BF16)
        found = lax.dot_general(
            fields, chosen, (((1,), (1,)), ((), ())), preferred_element_type=F32
        )
        lines[2 * place : 2 * place + 1, :MOST] = found[0:1]
        lines[2 * place : 2 * place + 1, MOST:] = found[1:2]
        lines[2 * place + 1 : 2 * place + 2, :MOST] = found[2:3]
        lines[2 * place + 1 : 2 * place + 2, MOST:] = found[3:4]
    out_ref[...] = lines[...].astype(BF16)


def product_table(x, a_index, b_index, live, owner, target):
    lists = [a_index, b_index, live, owner[:, 0], target]
    return pl.pallas_call(
        table_kernel,
        out_shape=jax.ShapeDtypeStruct((LABELS, 2 * MOST), BF16),
        in_specs=[SMEM] + [VMEM] * 5,
        out_specs=VMEM,
        scratch_shapes=[pltpu.VMEM((LABELS, 2 * MOST), F32)],
        cost_estimate=pl.CostEstimate(flops=TABLE_COST, bytes_accessed=1 << 16, transcendentals=0),
        name="product_table",
    )(x, *lists)


def spread_kernel(rep_ref, left_ref, *refs):
    outs, turned = refs[:N_REP], refs[N_REP]
    for pair in range(4):
        tile = left_ref[2 * pair : 2 * pair + 2].reshape(2 * QUARTER, TILE)
        turned[pair] = tile.T
    for shift in range(N_REP):
        to = lax.rem(rep_ref[0] + shift, N_REP)
        first = pl.multiple_of(to * QUARTER, QUARTER)
        for pair in range(4):
            outs[shift][pair] = turned[pair, pl.ds(first, QUARTER), :]


def spread_rows(rep, left):
    return pl.pallas_call(
        spread_kernel,
        out_shape=[jax.ShapeDtypeStruct((4, QUARTER, 2 * QUARTER), BF16)] * N_REP,
        in_specs=[SMEM, VMEM],
        out_specs=[VMEM] * N_REP,
        scratch_shapes=[pltpu.VMEM((4, TILE, 2 * QUARTER), BF16)],
        name="spread_rows",
    )(rep, left.transpose(0, 2, 1))


def join_kernel(table_ref, *refs):
    parts, out_ref = refs[:N_REP], refs[N_REP]
    for pair in range(4):
        pieces = [part[pair] for part in parts]
        for side in range(2):
            first = (2 * pair + side) * QUARTER
            out_ref[first : first + QUARTER] = jnp.concatenate(
                [p[:, QUARTER * side : QUARTER * (side + 1)] for p in pieces], axis=1
            )
    out_ref[ROWS:BLOCK] = table_ref[...]


def join_k(table, parts):
    return pl.pallas_call(
        join_kernel,
        out_shape=jax.ShapeDtypeStruct((BLOCK, TILE), BF16),
        in_specs=[VMEM] * (N_REP + 1),
        out_specs=VMEM,
        name="join_k",
    )(table, *parts)


def exact_dot(left, right):
    return jnp.dot(left.astype(F32).astype(BF16), right, preferred_element_type=F32)


def sort_kernel(me_ref, *refs):
    lefts, listed, fetched, labels, sems = refs[:N_SRC], *refs[N_SRC:]
    me = me_ref[0]
    tables = [
        pltpu.make_async_copy(lefts[i].at[pl.ds(ROWS, LABELS)], fetched.at[i], sems.at[i])
        for i in range(N_SRC)
    ]
    for copy in tables:
        copy.start()
    for copy in tables:
        copy.wait()
    labels[...] = fetched[...].astype(F32)
    rows = [labels[i, pl.ds(2 * me + half, 1), :] for half in range(2) for i in range(N_SRC)]
    first = jnp.concatenate(rows[:N_SRC], axis=0)
    second = jnp.concatenate(rows[N_SRC:], axis=0)
    spot, a, b, rank = first[:, :MOST], first[:, MOST:], second[:, :MOST], second[:, MOST:]
    lane = lax.broadcasted_iota(I32, (MOST, MOST), 1)
    row = lax.broadcasted_iota(I32, (MOST, MOST), 0)
    lane_f = lane.astype(F32)
    tile = jnp.where(spot > 0.0, b, float(NB)).T
    rank = rank.T
    of_tile = [(tile[:, i : i + 1] == lane_f).astype(F32).astype(BF16) for i in range(N_SRC)]
    ones = jnp.ones((N_SRC, MOST), F32)
    source = lax.broadcasted_iota(I32, (N_SRC, MOST), 0)
    sizes = jnp.zeros((N_SRC, MOST), F32)
    for i in range(N_SRC):
        sizes = jnp.where(source == i, exact_dot(ones, of_tile[i]), sizes)
    before, below = jnp.zeros((N_SRC, MOST), F32), jnp.zeros((1, MOST), F32)
    for i in range(N_SRC):
        before = jnp.where(source == i, below, before)
        below = below + sizes[i : i + 1]
    groups = jnp.floor((below + (GROUP - 1)) * (1.0 / GROUP))
    groups = jnp.where(lane[:1] < NB, groups, 0.0)
    high = jnp.floor(groups * (1.0 / 128.0))
    earlier = (row < lane).astype(F32).astype(BF16)
    starts = exact_dot(jnp.broadcast_to(groups - 128.0 * high, (N_SRC, MOST)), earlier)
    starts += 128.0 * exact_dot(jnp.broadcast_to(high, (N_SRC, MOST)), earlier)
    starts = GROUP * starts
    base = jnp.where(lane[:N_SRC] < NB, before + starts, 2.0 * LIST)
    high = jnp.floor(base * (1.0 / 128.0))
    low, high = (base - 128.0 * high).T, high.T
    places, fields = [], []
    for i in range(N_SRC):
        place = 128.0 * jnp.dot(of_tile[i], high.astype(BF16), preferred_element_type=F32)
        place += jnp.dot(of_tile[i], low.astype(BF16), preferred_element_type=F32)
        places.append(place[:, i : i + 1] + rank[:, i : i + 1])
        field = jnp.where(source == 0, spot[i : i + 1] - 1.0, a[i : i + 1] + 8.0 * i)
        field = jnp.where(source == 2, b[i : i + 1], field)
        fields.append(jnp.where(source == 3, 1.0, field).astype(BF16))
    for line in range(LIST // MOST):
        found = jnp.zeros((N_SRC, MOST), F32)
        for i in range(N_SRC):
            here = (places[i] == lane_f + float(line * MOST)).astype(F32).astype(BF16)
            found += jnp.dot(fields[i], here, preferred_element_type=F32)
        code = found[0:1] * 4096.0 + found[1:2] * 64.0 + found[2:3]
        code = jnp.where(found[3:4] > 0.0, code, NOWHERE)
        listed[line : line + 1, :] = code.astype(I32)
    listed[LIST // MOST : LIST // MOST + 1, :] = starts[:1].astype(I32)


def sort_products(me, lefts):
    return pl.pallas_call(
        sort_kernel,
        out_shape=jax.ShapeDtypeStruct((LIST // MOST + 1, MOST), I32),
        in_specs=[SMEM] + [ANY] * N_SRC,
        out_specs=VMEM,
        scratch_shapes=[
            pltpu.VMEM((N_SRC, LABELS, TILE), BF16),
            pltpu.VMEM((N_SRC, LABELS, TILE), F32),
            pltpu.SemaphoreType.DMA((N_SRC,)),
        ],
        cost_estimate=pl.CostEstimate(flops=SORT_COST, bytes_accessed=1 << 16, transcendentals=0),
        name="sort_products",
    )(me, *lefts)


N_RIGHT = 9


def products_kernel(me_ref, listed, *refs):
    lefts, rights, refs = refs[:N_SRC], refs[N_SRC : N_SRC + N_RIGHT], refs[N_SRC + N_RIGHT :]
    away_ref, home_ref, left, right, total, left_sems, right_sems = refs
    core = me_ref[1]
    copies = [
        pltpu.make_async_copy(lefts[i].at[pl.ds(0, ROWS)], left.at[i], left_sems.at[i])
        for i in range(N_SRC)
    ]
    copies.append(pltpu.make_async_copy(rights[0], right.at[0], right_sems.at[0]))
    i = 1
    for first in (core * HALF, (1 - core) * HALF):
        for quarter, skip, size in ((1, 0, HALF), (3, 0, HALF), (2, 0, HALF // 2), (2, HALF // 2, HALF // 2)):
            spot = right.at[quarter, pl.ds(pl.multiple_of(first + skip, HALF // 2), size)]
            copies.append(pltpu.make_async_copy(rights[i], spot, right_sems.at[i]))
            i += 1
    for copy in copies:
        copy.start()
    total[...] = jnp.zeros_like(total)
    for copy in copies:
        copy.wait()

    def step(i, carry):
        sums = []
        for w in range(WIDE):
            spots, rows = [], []
            for u in range(GROUP):
                at = (i % 4) * GROUP * WIDE + w * GROUP + u
                code = listed[i // 4, at]
                first = pl.multiple_of(((code >> 6) & 7) * QUARTER, QUARTER)
                rows.append(left[(code >> 9) & 7, pl.ds(first, QUARTER), :])
                spots.append(code >> 12)
                b = code & (NB - 1) if u == 0 else b
            tile = jnp.concatenate([right[q, b] for q in range(N_REP)], axis=0)
            lhs = jnp.concatenate(rows, axis=0)
            sums.append((spots, jnp.dot(lhs, tile, preferred_element_type=F32)))
        for spots, value in sums:
            for u in range(GROUP):
                total[spots[u]] += value[u * QUARTER : (u + 1) * QUARTER]
        return carry

    lax.fori_loop(0, (listed[LIST // MOST, NB] + GROUP * WIDE - 1) // (GROUP * WIDE), step, 0)
    home_ref[...] = total[pl.ds(pl.multiple_of(core * SPOTS, SPOTS), SPOTS)].astype(BF16)
    away_ref[...] = total[pl.ds(pl.multiple_of((1 - core) * SPOTS, SPOTS), SPOTS)].astype(BF16)


def products(me, listed, lefts, rights):
    shape = (SPOTS, QUARTER, TILE)
    return pl.pallas_call(
        products_kernel,
        out_shape=[jax.ShapeDtypeStruct(shape, BF16)] * 2,
        in_specs=[SMEM] * 2 + [ANY] * (N_SRC + N_RIGHT),
        out_specs=[VMEM] * 2,
        scratch_shapes=[
            pltpu.VMEM((N_SRC, ROWS, TILE), BF16),
            pltpu.VMEM((N_REP, NB, QUARTER, TILE), BF16),
            pltpu.VMEM((2 * SPOTS + 1, QUARTER, TILE), F32),
            pltpu.SemaphoreType.DMA((N_SRC,)),
            pltpu.SemaphoreType.DMA((N_RIGHT,)),
        ],
        compiler_params=pltpu.CompilerParams(vmem_limit_bytes=VMEM_LIMIT),
        cost_estimate=pl.CostEstimate(
            flops=2 * 384 * 64 * 256 * 256, bytes_accessed=10 << 20, transcendentals=0
        ),
        name="products",
    )(me, listed, *lefts, *rights)


def shift_by(value, axis, size, step):
    return lax.ppermute(value, axis, [(i, (i + step) % size) for i in range(size)])


def apart(value, axis, size):
    perm = []
    for i in range(size):
        perm.append((i * 2, ((i + 1) % size) * 2))
        perm.append((i * 2 + 1, ((i - 1) % size) * 2 + 1))
    return lax.ppermute(value, (axis, "core"), perm)


def other_core(value):
    return lax.ppermute(value, "core", [(0, 1), (1, 0)])


def gather(mine, half):
    back = shift_by(half, "rep", N_REP, 1)
    ahead = shift_by(half, "rep", N_REP, -1)
    own, other = mine, other_core(mine)
    blocks = [own]
    for distance in range(3):
        own, other = apart(own, "z", N_Z), apart(other, "z", N_Z)
        blocks += [own, other]
    far_back = shift_by(back[: HALF // 2], "rep", N_REP, 1)
    far_ahead = shift_by(ahead[HALF // 2 :], "rep", N_REP, -1)
    parts = [back, ahead, far_back, far_ahead]
    return blocks + [apart(own, "z", N_Z)], parts + [other_core(part) for part in parts]


def body(amps, integrals, a_index, b_index, live, owner, target):
    rep, z, x, core = [lax.axis_index(n).astype(I32) for n in ("rep", "z", "x", "core")]
    x, *pieces = lax.optimization_barrier((x, *spread_rows(rep[None], amps)))
    half = lax.dynamic_slice_in_dim(integrals, core * HALF, HALF, 0)
    table = product_table(x[None], a_index, b_index, live, owner, target)
    parts = [pieces[0]] + [shift_by(pieces[s], "rep", N_REP, s) for s in range(1, N_REP)]
    half, table, *parts = lax.optimization_barrier((half, table, *parts))
    lefts, rights = gather(join_k(table, parts), half)
    me = jnp.stack([z, core])
    away, home = products(me, sort_products(me, lefts), lefts, [integrals] + rights)
    sums = home.astype(F32) + other_core(away).astype(F32)
    sums = sums.reshape(N_X, OWN_DEV, QUARTER, TILE)
    total = sums[0]
    for step in range(1, N_X):
        total = total + shift_by(sums[step].astype(BF16), "x", N_X, step).astype(F32)
    return total


def solution(mesh):
    devices = mesh.devices.reshape(N_REP, N_Z, N_X, N_CORE)
    fine = Mesh(devices, ("rep", "z", "x", "core"))
    task = ("z", "x", "core")
    in_specs = (
        P(task, None, "rep"),
        P(None, "rep", None),
        P(task),
        P(task),
        P(task),
        P(task, None),
        P(task),
    )
    return jax.shard_map(
        body, mesh=fine, in_specs=in_specs, out_specs=P(task, "rep", None), check_vma=False
    )
```

```python
import jax
import jax.numpy as jnp
from jax import lax
from jax.experimental import pallas as pl
from jax.experimental.pallas import tpu as pltpu
from jax.sharding import Mesh
from jax.sharding import PartitionSpec as P

N_REP, N_Z, N_X, N_CORE = 4, 8, 4, 2
N_SRC = N_Z
A_DEV = 8
OWN_DEV = 8
TPS = 8
NB = 64
HALF = NB // 2
PART = HALF // 2
QUARTER = 64
TILE = 256
MOST = 128
LABELS = 2 * N_Z
SPOTS = N_X * OWN_DEV
GROUP = 4
WIDE = 8
LIST = 1280
NOWHERE = 2.0 * SPOTS * 4096
SORT_COST = 20 * 10**9
ROWS = A_DEV * QUARTER
BLOCK = ROWS + LABELS
TABLE_COST = 4 * 10**9
VMEM_LIMIT = 56 * 1024 * 1024
BF16 = jnp.bfloat16
F32 = jnp.float32
I32 = jnp.int32
VMEM = pl.BlockSpec(memory_space=pltpu.VMEM)
SMEM = pl.BlockSpec(memory_space=pltpu.SMEM)
ANY = pl.BlockSpec(memory_space=pl.ANY)


def table_kernel(x_ref, a_ref, b_ref, live_ref, owner_ref, target_ref, out_ref, lines):
    products, slots = a_ref.shape[0], owner_ref.shape[0]
    x = x_ref[0]
    row = lax.broadcasted_iota(I32, (8, slots), 0)
    named = jnp.where(row == 0, owner_ref[...][None], jnp.where(row == 1, target_ref[...][None], 0))
    slot = lax.broadcasted_iota(I32, (slots, products), 0)
    spread = lax.broadcasted_iota(I32, (slots, products), 1) // TPS == slot
    named = jnp.dot(named.astype(F32), spread.astype(F32), precision=lax.Precision.HIGHEST)
    own, target = named[0:1].astype(I32), named[1:2].astype(I32)
    a, b = a_ref[...][None], b_ref[...][None]
    place = jnp.where(live_ref[...][None] > 0, own // (N_X * N_CORE), -1)
    spot = own % N_CORE * SPOTS + ((own // N_CORE - x) & (N_X - 1)) * OWN_DEV + target + 1
    row = lax.broadcasted_iota(I32, (8, products), 0)
    turned = jnp.where(row == 0, place, b).astype(F32).T
    same = turned[:, 0:1] == place.astype(F32)
    order = lax.broadcasted_iota(I32, (products, products), 0)
    same = same & (order < lax.broadcasted_iota(I32, (products, products), 1))
    alike = same & (turned[:, 1:2] == b.astype(F32))
    standing = jnp.sum(same.astype(F32), axis=0, keepdims=True).astype(I32)
    rank = jnp.sum(alike.astype(F32), axis=0, keepdims=True).astype(I32)
    at = jnp.where(place >= 0, place * MOST + standing, -1)
    fields = jnp.where(row == 0, spot, jnp.where(row == 1, a, jnp.where(row == 2, b, rank)))
    fields = fields.astype(F32).astype(BF16)
    position = lax.broadcasted_iota(I32, (MOST, products), 0)
    for place in range(N_Z):
        chosen = (at == position + place * MOST).astype(F32).astype(BF16)
        found = lax.dot_general(
            fields, chosen, (((1,), (1,)), ((), ())), preferred_element_type=F32
        )
        lines[2 * place : 2 * place + 1, :MOST] = found[0:1]
        lines[2 * place : 2 * place + 1, MOST:] = found[1:2]
        lines[2 * place + 1 : 2 * place + 2, :MOST] = found[2:3]
        lines[2 * place + 1 : 2 * place + 2, MOST:] = found[3:4]
    out_ref[...] = lines[...].astype(BF16)


def product_table(x, a_index, b_index, live, owner, target):
    lists = [a_index, b_index, live, owner[:, 0], target]
    return pl.pallas_call(
        table_kernel,
        out_shape=jax.ShapeDtypeStruct((LABELS, 2 * MOST), BF16),
        in_specs=[SMEM] + [VMEM] * 5,
        out_specs=VMEM,
        scratch_shapes=[pltpu.VMEM((LABELS, 2 * MOST), F32)],
        cost_estimate=pl.CostEstimate(flops=TABLE_COST, bytes_accessed=1 << 16, transcendentals=0),
        name="product_table",
    )(x, *lists)


def spread_kernel(rep_ref, left_ref, *refs):
    outs, turned = refs[:N_REP], refs[N_REP]
    for pair in range(4):
        tile = left_ref[2 * pair : 2 * pair + 2].reshape(2 * QUARTER, TILE)
        turned[pair] = tile.T
    for shift in range(N_REP):
        to = lax.rem(rep_ref[0] + shift, N_REP)
        first = pl.multiple_of(to * QUARTER, QUARTER)
        for pair in range(4):
            outs[shift][pair] = turned[pair, pl.ds(first, QUARTER), :]


def spread_rows(rep, left):
    return pl.pallas_call(
        spread_kernel,
        out_shape=[jax.ShapeDtypeStruct((4, QUARTER, 2 * QUARTER), BF16)] * N_REP,
        in_specs=[SMEM, VMEM],
        out_specs=[VMEM] * N_REP,
        scratch_shapes=[pltpu.VMEM((4, TILE, 2 * QUARTER), BF16)],
        name="spread_rows",
    )(rep, left.transpose(0, 2, 1))


def join_kernel(table_ref, *refs):
    parts, out_ref = refs[:N_REP], refs[N_REP]
    for pair in range(4):
        pieces = [part[pair] for part in parts]
        for side in range(2):
            first = (2 * pair + side) * QUARTER
            out_ref[first : first + QUARTER] = jnp.concatenate(
                [p[:, QUARTER * side : QUARTER * (side + 1)] for p in pieces], axis=1
            )
    out_ref[ROWS:BLOCK] = table_ref[...]


def join_k(table, parts):
    return pl.pallas_call(
        join_kernel,
        out_shape=jax.ShapeDtypeStruct((BLOCK, TILE), BF16),
        in_specs=[VMEM] * (N_REP + 1),
        out_specs=VMEM,
        name="join_k",
    )(table, *parts)


def exact_dot(left, right):
    return jnp.dot(left.astype(F32).astype(BF16), right, preferred_element_type=F32)


def sort_kernel(me_ref, *refs):
    lefts, listed, fetched, labels, sems = refs[:N_SRC], *refs[N_SRC:]
    me = me_ref[0]
    tables = [
        pltpu.make_async_copy(lefts[i].at[pl.ds(ROWS, LABELS)], fetched.at[i], sems.at[i])
        for i in range(N_SRC)
    ]
    for copy in tables:
        copy.start()
    for copy in tables:
        copy.wait()
    labels[...] = fetched[...].astype(F32)
    rows = [labels[i, pl.ds(2 * me + half, 1), :] for half in range(2) for i in range(N_SRC)]
    first = jnp.concatenate(rows[:N_SRC], axis=0)
    second = jnp.concatenate(rows[N_SRC:], axis=0)
    spot, a, b, rank = first[:, :MOST], first[:, MOST:], second[:, :MOST], second[:, MOST:]
    b += (me_ref[1] * HALF).astype(F32)
    b = jnp.where(b < NB, b, b - NB)
    lane = lax.broadcasted_iota(I32, (MOST, MOST), 1)
    row = lax.broadcasted_iota(I32, (MOST, MOST), 0)
    lane_f = lane.astype(F32)
    tile = jnp.where(spot > 0.0, b, float(NB)).T
    rank = rank.T
    of_tile = [(tile[:, i : i + 1] == lane_f).astype(F32).astype(BF16) for i in range(N_SRC)]
    ones = jnp.ones((N_SRC, MOST), F32)
    source = lax.broadcasted_iota(I32, (N_SRC, MOST), 0)
    sizes = jnp.zeros((N_SRC, MOST), F32)
    for i in range(N_SRC):
        sizes = jnp.where(source == i, exact_dot(ones, of_tile[i]), sizes)
    before, below = jnp.zeros((N_SRC, MOST), F32), jnp.zeros((1, MOST), F32)
    for i in range(N_SRC):
        before = jnp.where(source == i, below, before)
        below = below + sizes[i : i + 1]
    groups = jnp.floor((below + (GROUP - 1)) * (1.0 / GROUP))
    groups = jnp.where(lane[:1] < NB, groups, 0.0)
    high = jnp.floor(groups * (1.0 / 128.0))
    earlier = (row < lane).astype(F32).astype(BF16)
    starts = exact_dot(jnp.broadcast_to(groups - 128.0 * high, (N_SRC, MOST)), earlier)
    starts += 128.0 * exact_dot(jnp.broadcast_to(high, (N_SRC, MOST)), earlier)
    starts = GROUP * starts
    base = jnp.where(lane[:N_SRC] < NB, before + starts, 2.0 * LIST)
    high = jnp.floor(base * (1.0 / 128.0))
    low, high = (base - 128.0 * high).T, high.T
    places, fields = [], []
    for i in range(N_SRC):
        place = 128.0 * jnp.dot(of_tile[i], high.astype(BF16), preferred_element_type=F32)
        place += jnp.dot(of_tile[i], low.astype(BF16), preferred_element_type=F32)
        places.append(place[:, i : i + 1] + rank[:, i : i + 1])
        field = jnp.where(source == 0, spot[i : i + 1] - 1.0, a[i : i + 1] + 8.0 * i)
        field = jnp.where(source == 2, b[i : i + 1], field)
        fields.append(jnp.where(source == 3, 1.0, field).astype(BF16))
    field = jnp.concatenate(fields, axis=1)

    def fill(line):
        here = [(place == lane_f + float(line * MOST)).astype(F32).astype(BF16) for place in places]
        found = jnp.dot(field, jnp.concatenate(here, axis=0), preferred_element_type=F32)
        code = found[0:1] * 4096.0 + found[1:2] * 64.0 + found[2:3]
        code = jnp.where(found[3:4] > 0.0, code, NOWHERE)
        listed[line : line + 1, :] = code.astype(I32)

    for line in range(LIST // MOST // 2):
        fill(line)

    @pl.when(jnp.max(starts) > LIST // 2)
    def _():
        for line in range(LIST // MOST // 2, LIST // MOST):
            fill(line)

    listed[LIST // MOST : LIST // MOST + 1, :] = starts[:1].astype(I32)


def sort_products(me, lefts):
    return pl.pallas_call(
        sort_kernel,
        out_shape=jax.ShapeDtypeStruct((LIST // MOST + 1, MOST), I32),
        in_specs=[SMEM] + [ANY] * N_SRC,
        out_specs=VMEM,
        scratch_shapes=[
            pltpu.VMEM((N_SRC, LABELS, TILE), BF16),
            pltpu.VMEM((N_SRC, LABELS, TILE), F32),
            pltpu.SemaphoreType.DMA((N_SRC,)),
        ],
        cost_estimate=pl.CostEstimate(flops=SORT_COST, bytes_accessed=1 << 16, transcendentals=0),
        name="sort_products",
    )(me, *lefts)


STEPS = NB // PART
N_RIGHT = 9


def products_kernel(me_ref, listed, *refs):
    lefts, rights, refs = refs[:N_SRC], refs[N_SRC : N_SRC + N_RIGHT], refs[N_SRC + N_RIGHT :]
    away_refs, home_refs, refs = refs[:N_X], refs[N_X : 2 * N_X], refs[2 * N_X :]
    left, right, total, left_sems, right_sems = refs
    core = me_ref[1]
    copies = [
        pltpu.make_async_copy(lefts[i].at[pl.ds(0, ROWS)], left.at[i], left_sems.at[i])
        for i in range(N_SRC)
    ]
    fetches = []
    for step in range(STEPS):
        first = (core * HALF + step * PART) & (NB - 1)
        back, far_back, far_ahead, ahead = rights[1 + step // 2 * 4 : 5 + step // 2 * 4]
        side = pl.ds(step % 2 * PART, PART)
        sources = [
            rights[0].at[pl.ds(pl.multiple_of(first, PART), PART)],
            back.at[side],
            far_ahead if step % 2 else far_back,
            ahead.at[side],
        ]
        fetches.append(
            [
                pltpu.make_async_copy(
                    source, right.at[q, pl.ds(step * PART, PART)], right_sems.at[4 * step + q]
                )
                for q, source in enumerate(sources)
            ]
        )
    for copy in copies + fetches[0]:
        copy.start()
    total[...] = jnp.zeros_like(total)
    for copy in copies:
        copy.wait()
    for fetch in fetches[1]:
        fetch.start()

    def step(i, carry):
        sums = []
        for w in range(WIDE):
            spots, rows = [], []
            for u in range(GROUP):
                at = (i % 4) * GROUP * WIDE + w * GROUP + u
                code = listed[i // 4, at]
                first = pl.multiple_of(((code >> 6) & 7) * QUARTER, QUARTER)
                rows.append(left[(code >> 9) & 7, pl.ds(first, QUARTER), :])
                spots.append(code >> 12)
                b = code & (NB - 1) if u == 0 else b
            tile = jnp.concatenate([right[q, b] for q in range(N_REP)], axis=0)
            lhs = jnp.concatenate(rows, axis=0)
            sums.append((spots, jnp.dot(lhs, tile, preferred_element_type=F32)))
        for spots, value in sums:
            for u in range(GROUP):
                total[spots[u]] += value[u * QUARTER : (u + 1) * QUARTER]
        return carry

    done = 0
    for part in range(STEPS):
        for fetch in fetches[part]:
            fetch.wait()
        if part + 2 < STEPS:
            for fetch in fetches[part + 2]:
                fetch.start()
        end = listed[LIST // MOST, (part + 1) * PART]
        end = end // (GROUP * WIDE) if part < STEPS - 1 else (end + GROUP * WIDE - 1) // (GROUP * WIDE)
        lax.fori_loop(done, end, step, 0)
        done = end
    for refs, owner_core in ((away_refs, 1 - core), (home_refs, core)):
        for shift, ref in enumerate(refs):
            first = pl.multiple_of(owner_core * SPOTS + shift * OWN_DEV, OWN_DEV)
            ref[...] = total[pl.ds(first, OWN_DEV)].astype(ref.dtype)


def products(me, listed, lefts, rights):
    shape = (OWN_DEV, QUARTER, TILE)
    types = [BF16] * N_X + [F32] + [BF16] * (N_X - 1)
    return pl.pallas_call(
        products_kernel,
        out_shape=[jax.ShapeDtypeStruct(shape, kind) for kind in types],
        in_specs=[SMEM] * 2 + [ANY] * (N_SRC + N_RIGHT),
        out_specs=[VMEM] * (2 * N_X),
        scratch_shapes=[
            pltpu.VMEM((N_SRC, ROWS, TILE), BF16),
            pltpu.VMEM((N_REP, NB, QUARTER, TILE), BF16),
            pltpu.VMEM((2 * SPOTS + 1, QUARTER, TILE), F32),
            pltpu.SemaphoreType.DMA((N_SRC,)),
            pltpu.SemaphoreType.DMA((N_REP * STEPS,)),
        ],
        compiler_params=pltpu.CompilerParams(vmem_limit_bytes=VMEM_LIMIT),
        cost_estimate=pl.CostEstimate(
            flops=2 * 384 * 64 * 256 * 256, bytes_accessed=10 << 20, transcendentals=0
        ),
        name="products",
    )(me, listed, *lefts, *rights)


def shift_by(value, axis, size, step):
    return lax.ppermute(value, axis, [(i, (i + step) % size) for i in range(size)])


def apart(value, axis, size):
    perm = []
    for i in range(size):
        perm.append((i * 2, ((i + 1) % size) * 2))
        perm.append((i * 2 + 1, ((i - 1) % size) * 2 + 1))
    return lax.ppermute(value, (axis, "core"), perm)


def other_core(value):
    return lax.ppermute(value, "core", [(0, 1), (1, 0)])


def gather(mine, half):
    back = shift_by(half, "rep", N_REP, 1)
    ahead = shift_by(half, "rep", N_REP, -1)
    own, other = mine, other_core(mine)
    blocks = [own]
    for distance in range(3):
        own, other = apart(own, "z", N_Z), apart(other, "z", N_Z)
        blocks += [own, other]
    far_back = shift_by(back[: HALF // 2], "rep", N_REP, 1)
    far_ahead = shift_by(ahead[HALF // 2 :], "rep", N_REP, -1)
    parts = [back, far_back, far_ahead, ahead]
    return blocks + [apart(own, "z", N_Z)], parts + [other_core(part) for part in parts]


def body(amps, integrals, a_index, b_index, live, owner, target):
    rep, z, x, core = [lax.axis_index(n).astype(I32) for n in ("rep", "z", "x", "core")]
    x, *pieces = lax.optimization_barrier((x, *spread_rows(rep[None], amps)))
    half = lax.dynamic_slice_in_dim(integrals, core * HALF, HALF, 0)
    table = product_table(x[None], a_index, b_index, live, owner, target)
    parts = [pieces[0]] + [shift_by(pieces[s], "rep", N_REP, s) for s in range(1, N_REP)]
    joined, half = lax.optimization_barrier((join_k(table, parts), half))
    lefts, rights = gather(joined, half)
    me = jnp.stack([z, core])
    sums = products(me, sort_products(me, lefts), lefts, [integrals] + rights)
    total = None
    for shift in (2, 1, 3, 0):
        part = sums[N_X + shift].astype(F32) + other_core(sums[shift]).astype(F32)
        if shift > 0:
            part = shift_by(part.astype(BF16), "x", N_X, shift).astype(F32)
        total = part if total is None else total + part
    return total


def solution(mesh):
    devices = mesh.devices.reshape(N_REP, N_Z, N_X, N_CORE)
    fine = Mesh(devices, ("rep", "z", "x", "core"))
    task = ("z", "x", "core")
    in_specs = (
        P(task, None, "rep"),
        P(None, "rep", None),
        P(task),
        P(task),
        P(task),
        P(task, None),
        P(task),
    )
    return jax.shard_map(
        body, mesh=fine, in_specs=in_specs, out_specs=P(task, "rep", None), check_vma=False
    )
```

```python
import jax
import jax.numpy as jnp
from jax import lax
from jax.experimental import pallas as pl
from jax.experimental.pallas import tpu as pltpu
from jax.sharding import Mesh
from jax.sharding import PartitionSpec as P

N_REP, N_Z, N_X, N_CORE = 4, 8, 4, 2
N_SRC = N_Z
A_DEV = 8
OWN_DEV = 8
TPS = 8
NB = 64
HALF = NB // 2
PART = HALF // 2
QUARTER = 64
TILE = 256
MOST = 128
LABELS = 2 * N_Z
SPOTS = N_X * OWN_DEV
GROUP = 4
WIDE = 8
LIST = 1280
NOWHERE = 2.0 * SPOTS * 4096
SORT_COST = 20 * 10**9
ROWS = A_DEV * QUARTER
BLOCK = ROWS + LABELS
JOIN_COST = 20 * 10**9
TABLE_COST = 8 * 10**9
VMEM_LIMIT = 56 * 1024 * 1024
BF16 = jnp.bfloat16
F32 = jnp.float32
I32 = jnp.int32
VMEM = pl.BlockSpec(memory_space=pltpu.VMEM)
SMEM = pl.BlockSpec(memory_space=pltpu.SMEM)
ANY = pl.BlockSpec(memory_space=pl.ANY)


def table_kernel(x_ref, a_ref, b_ref, live_ref, owner_ref, target_ref, out_ref, lines):
    products, slots = a_ref.shape[0], owner_ref.shape[0]
    x = x_ref[0]
    row = lax.broadcasted_iota(I32, (8, slots), 0)
    named = jnp.where(row == 0, owner_ref[...][None], jnp.where(row == 1, target_ref[...][None], 0))
    slot = lax.broadcasted_iota(I32, (slots, products), 0)
    spread = lax.broadcasted_iota(I32, (slots, products), 1) // TPS == slot
    named = jnp.dot(named.astype(F32), spread.astype(F32), precision=lax.Precision.HIGHEST)
    own, target = named[0:1].astype(I32), named[1:2].astype(I32)
    a, b = a_ref[...][None], b_ref[...][None]
    place = jnp.where(live_ref[...][None] > 0, own // (N_X * N_CORE), -1)
    spot = own % N_CORE * SPOTS + ((own // N_CORE - x) & (N_X - 1)) * OWN_DEV + target + 1
    row = lax.broadcasted_iota(I32, (8, products), 0)
    turned = jnp.where(row == 0, place, b).astype(F32).T
    same = turned[:, 0:1] == place.astype(F32)
    order = lax.broadcasted_iota(I32, (products, products), 0)
    same = same & (order < lax.broadcasted_iota(I32, (products, products), 1))
    alike = same & (turned[:, 1:2] == b.astype(F32))
    standing = jnp.sum(same.astype(F32), axis=0, keepdims=True).astype(I32)
    rank = jnp.sum(alike.astype(F32), axis=0, keepdims=True).astype(I32)
    at = jnp.where(place >= 0, place * MOST + standing, -1)
    fields = jnp.where(row == 0, spot, jnp.where(row == 1, a, jnp.where(row == 2, b, rank)))
    fields = fields.astype(F32).astype(BF16)
    position = lax.broadcasted_iota(I32, (MOST, products), 0)
    for place in range(N_Z):
        chosen = (at == position + place * MOST).astype(F32).astype(BF16)
        found = lax.dot_general(
            fields, chosen, (((1,), (1,)), ((), ())), preferred_element_type=F32
        )
        lines[2 * place : 2 * place + 1, :MOST] = found[0:1]
        lines[2 * place : 2 * place + 1, MOST:] = found[1:2]
        lines[2 * place + 1 : 2 * place + 2, :MOST] = found[2:3]
        lines[2 * place + 1 : 2 * place + 2, MOST:] = found[3:4]
    out_ref[...] = lines[...].astype(BF16)


def product_table(x, a_index, b_index, live, owner, target):
    lists = [a_index, b_index, live, owner[:, 0], target]
    return pl.pallas_call(
        table_kernel,
        out_shape=jax.ShapeDtypeStruct((LABELS, 2 * MOST), BF16),
        in_specs=[SMEM] + [VMEM] * 5,
        out_specs=VMEM,
        scratch_shapes=[pltpu.VMEM((LABELS, 2 * MOST), F32)],
        cost_estimate=pl.CostEstimate(flops=TABLE_COST, bytes_accessed=1 << 16, transcendentals=0),
        name="product_table",
    )(x, *lists)


def spread_kernel(rep_ref, left_ref, *refs):
    outs, turned = refs[:N_REP], refs[N_REP]
    for pair in range(4):
        tile = left_ref[2 * pair : 2 * pair + 2].reshape(2 * QUARTER, TILE)
        turned[pair] = tile.T
    for shift in range(N_REP):
        to = lax.rem(rep_ref[0] + shift, N_REP)
        first = pl.multiple_of(to * QUARTER, QUARTER)
        for pair in range(4):
            outs[shift][pair] = turned[pair, pl.ds(first, QUARTER), :]


def spread_rows(rep, left):
    return pl.pallas_call(
        spread_kernel,
        out_shape=[jax.ShapeDtypeStruct((4, QUARTER, 2 * QUARTER), BF16)] * N_REP,
        in_specs=[SMEM, VMEM],
        out_specs=[VMEM] * N_REP,
        scratch_shapes=[pltpu.VMEM((4, TILE, 2 * QUARTER), BF16)],
        name="spread_rows",
    )(rep, left.transpose(0, 2, 1))


def join_kernel(table_ref, *refs):
    parts, out_ref = refs[:N_REP], refs[N_REP]
    for pair in range(4):
        pieces = [part[pair] for part in parts]
        for side in range(2):
            first = (2 * pair + side) * QUARTER
            out_ref[first : first + QUARTER] = jnp.concatenate(
                [p[:, QUARTER * side : QUARTER * (side + 1)] for p in pieces], axis=1
            )
    out_ref[ROWS:BLOCK] = table_ref[...]


def join_k(table, parts):
    return pl.pallas_call(
        join_kernel,
        out_shape=jax.ShapeDtypeStruct((BLOCK, TILE), BF16),
        in_specs=[VMEM] * (N_REP + 1),
        out_specs=VMEM,
        cost_estimate=pl.CostEstimate(flops=JOIN_COST, bytes_accessed=1 << 19, transcendentals=0),
        name="join_k",
    )(table, *parts)


def exact_dot(left, right):
    return jnp.dot(left.astype(F32).astype(BF16), right, preferred_element_type=F32)


def sort_kernel(me_ref, *refs):
    lefts, listed, fetched, labels, sems = refs[:N_SRC], *refs[N_SRC:]
    me = me_ref[0]
    tables = [
        pltpu.make_async_copy(lefts[i].at[pl.ds(ROWS, LABELS)], fetched.at[i], sems.at[i])
        for i in range(N_SRC)
    ]
    for copy in tables:
        copy.start()
    for copy in tables:
        copy.wait()
    labels[...] = fetched[...].astype(F32)
    rows = [labels[i, pl.ds(2 * me + half, 1), :] for half in range(2) for i in range(N_SRC)]
    first = jnp.concatenate(rows[:N_SRC], axis=0)
    second = jnp.concatenate(rows[N_SRC:], axis=0)
    spot, a, b, rank = first[:, :MOST], first[:, MOST:], second[:, :MOST], second[:, MOST:]
    b += (me_ref[1] * HALF).astype(F32)
    b = jnp.where(b < NB, b, b - NB)
    lane = lax.broadcasted_iota(I32, (MOST, MOST), 1)
    row = lax.broadcasted_iota(I32, (MOST, MOST), 0)
    lane_f = lane.astype(F32)
    tile = jnp.where(spot > 0.0, b, float(NB)).T
    rank = rank.T
    of_tile = [(tile[:, i : i + 1] == lane_f).astype(F32).astype(BF16) for i in range(N_SRC)]
    ones = jnp.ones((N_SRC, MOST), F32)
    source = lax.broadcasted_iota(I32, (N_SRC, MOST), 0)
    sizes = jnp.zeros((N_SRC, MOST), F32)
    for i in range(N_SRC):
        sizes = jnp.where(source == i, exact_dot(ones, of_tile[i]), sizes)
    before, below = jnp.zeros((N_SRC, MOST), F32), jnp.zeros((1, MOST), F32)
    for i in range(N_SRC):
        before = jnp.where(source == i, below, before)
        below = below + sizes[i : i + 1]
    groups = jnp.floor((below + (GROUP - 1)) * (1.0 / GROUP))
    groups = jnp.where(lane[:1] < NB, groups, 0.0)
    high = jnp.floor(groups * (1.0 / 128.0))
    earlier = (row < lane).astype(F32).astype(BF16)
    starts = exact_dot(jnp.broadcast_to(groups - 128.0 * high, (N_SRC, MOST)), earlier)
    starts += 128.0 * exact_dot(jnp.broadcast_to(high, (N_SRC, MOST)), earlier)
    starts = GROUP * starts
    base = jnp.where(lane[:N_SRC] < NB, before + starts, 2.0 * LIST)
    high = jnp.floor(base * (1.0 / 128.0))
    low, high = (base - 128.0 * high).T, high.T
    places, fields = [], []
    for i in range(N_SRC):
        place = 128.0 * jnp.dot(of_tile[i], high.astype(BF16), preferred_element_type=F32)
        place += jnp.dot(of_tile[i], low.astype(BF16), preferred_element_type=F32)
        places.append(place[:, i : i + 1] + rank[:, i : i + 1])
        field = jnp.where(source == 0, spot[i : i + 1] - 1.0, a[i : i + 1] + 8.0 * i)
        field = jnp.where(source == 2, b[i : i + 1], field)
        fields.append(jnp.where(source == 3, 1.0, field).astype(BF16))
    field = jnp.concatenate(fields, axis=1)

    def fill(line):
        here = [(place == lane_f + float(line * MOST)).astype(F32).astype(BF16) for place in places]
        found = jnp.dot(field, jnp.concatenate(here, axis=0), preferred_element_type=F32)
        code = found[0:1] * 4096.0 + found[1:2] * 64.0 + found[2:3]
        code = jnp.where(found[3:4] > 0.0, code, NOWHERE)
        listed[line : line + 1, :] = code.astype(I32)

    for line in range(LIST // MOST // 2):
        fill(line)

    @pl.when(jnp.max(starts) > LIST // 2)
    def _():
        for line in range(LIST // MOST // 2, LIST // MOST):
            fill(line)

    listed[LIST // MOST : LIST // MOST + 1, :] = starts[:1].astype(I32)


def sort_products(me, lefts):
    return pl.pallas_call(
        sort_kernel,
        out_shape=jax.ShapeDtypeStruct((LIST // MOST + 1, MOST), I32),
        in_specs=[SMEM] + [ANY] * N_SRC,
        out_specs=VMEM,
        scratch_shapes=[
            pltpu.VMEM((N_SRC, LABELS, TILE), BF16),
            pltpu.VMEM((N_SRC, LABELS, TILE), F32),
            pltpu.SemaphoreType.DMA((N_SRC,)),
        ],
        cost_estimate=pl.CostEstimate(flops=SORT_COST, bytes_accessed=1 << 16, transcendentals=0),
        name="sort_products",
    )(me, *lefts)


STEPS = NB // PART
N_RIGHT = 9


def products_kernel(me_ref, listed, *refs):
    lefts, rights, refs = refs[:N_SRC], refs[N_SRC : N_SRC + N_RIGHT], refs[N_SRC + N_RIGHT :]
    away_refs, home_refs, refs = refs[:N_X], refs[N_X : 2 * N_X], refs[2 * N_X :]
    left, right, total, left_sems, right_sems = refs
    core = me_ref[1]
    copies = [
        pltpu.make_async_copy(lefts[i].at[pl.ds(0, ROWS)], left.at[i], left_sems.at[i])
        for i in range(N_SRC)
    ]
    fetches = []
    for step in range(STEPS):
        first = (core * HALF + step * PART) & (NB - 1)
        back, far_back, far_ahead, ahead = rights[1 + step // 2 * 4 : 5 + step // 2 * 4]
        side = pl.ds(step % 2 * PART, PART)
        sources = [
            rights[0].at[pl.ds(pl.multiple_of(first, PART), PART)],
            back.at[side],
            far_ahead if step % 2 else far_back,
            ahead.at[side],
        ]
        fetches.append(
            [
                pltpu.make_async_copy(
                    source, right.at[q, pl.ds(step * PART, PART)], right_sems.at[4 * step + q]
                )
                for q, source in enumerate(sources)
            ]
        )
    for copy in copies + fetches[0]:
        copy.start()
    total[...] = jnp.zeros_like(total)
    for copy in copies:
        copy.wait()
    for fetch in fetches[1]:
        fetch.start()

    def step(i, carry):
        sums = []
        for w in range(WIDE):
            spots, rows = [], []
            for u in range(GROUP):
                at = (i % 4) * GROUP * WIDE + w * GROUP + u
                code = listed[i // 4, at]
                first = pl.multiple_of(((code >> 6) & 7) * QUARTER, QUARTER)
                rows.append(left[(code >> 9) & 7, pl.ds(first, QUARTER), :])
                spots.append(code >> 12)
                b = code & (NB - 1) if u == 0 else b
            tile = jnp.concatenate([right[q, b] for q in range(N_REP)], axis=0)
            lhs = jnp.concatenate(rows, axis=0)
            sums.append((spots, jnp.dot(lhs, tile, preferred_element_type=F32)))
        for spots, value in sums:
            for u in range(GROUP):
                total[spots[u]] += value[u * QUARTER : (u + 1) * QUARTER]
        return carry

    done = 0
    for part in range(STEPS):
        for fetch in fetches[part]:
            fetch.wait()
        if part + 2 < STEPS:
            for fetch in fetches[part + 2]:
                fetch.start()
        end = listed[LIST // MOST, (part + 1) * PART]
        end = end // (GROUP * WIDE) if part < STEPS - 1 else (end + GROUP * WIDE - 1) // (GROUP * WIDE)
        lax.fori_loop(done, end, step, 0)
        done = end
    for refs, owner_core in ((away_refs, 1 - core), (home_refs, core)):
        for shift, ref in enumerate(refs):
            first = pl.multiple_of(owner_core * SPOTS + shift * OWN_DEV, OWN_DEV)
            ref[...] = total[pl.ds(first, OWN_DEV)].astype(ref.dtype)


def products(me, listed, lefts, rights):
    shape = (OWN_DEV, QUARTER, TILE)
    types = [BF16] * N_X + [F32] + [BF16] * (N_X - 1)
    return pl.pallas_call(
        products_kernel,
        out_shape=[jax.ShapeDtypeStruct(shape, kind) for kind in types],
        in_specs=[SMEM] * 2 + [ANY] * (N_SRC + N_RIGHT),
        out_specs=[VMEM] * (2 * N_X),
        scratch_shapes=[
            pltpu.VMEM((N_SRC, ROWS, TILE), BF16),
            pltpu.VMEM((N_REP, NB, QUARTER, TILE), BF16),
            pltpu.VMEM((2 * SPOTS + 1, QUARTER, TILE), F32),
            pltpu.SemaphoreType.DMA((N_SRC,)),
            pltpu.SemaphoreType.DMA((N_REP * STEPS,)),
        ],
        compiler_params=pltpu.CompilerParams(vmem_limit_bytes=VMEM_LIMIT),
        cost_estimate=pl.CostEstimate(
            flops=2 * 384 * 64 * 256 * 256, bytes_accessed=10 << 20, transcendentals=0
        ),
        name="products",
    )(me, listed, *lefts, *rights)


def shift_by(value, axis, size, step):
    return lax.ppermute(value, axis, [(i, (i + step) % size) for i in range(size)])


def apart(value, axis, size):
    perm = []
    for i in range(size):
        perm.append((i * 2, ((i + 1) % size) * 2))
        perm.append((i * 2 + 1, ((i - 1) % size) * 2 + 1))
    return lax.ppermute(value, (axis, "core"), perm)


def other_core(value):
    return lax.ppermute(value, "core", [(0, 1), (1, 0)])


def gather(mine, half):
    back = shift_by(half, "rep", N_REP, 1)
    ahead = shift_by(half, "rep", N_REP, -1)
    own, other = mine, other_core(mine)
    blocks = [own]
    for distance in range(3):
        own, other = apart(own, "z", N_Z), apart(other, "z", N_Z)
        blocks += [own, other]
    far_back = shift_by(back[: HALF // 2], "rep", N_REP, 1)
    far_ahead = shift_by(ahead[HALF // 2 :], "rep", N_REP, -1)
    parts = [back, far_back, far_ahead, ahead]
    return blocks + [apart(own, "z", N_Z)], parts + [other_core(part) for part in parts]


def body(amps, integrals, a_index, b_index, live, owner, target):
    rep, z, x, core = [lax.axis_index(n).astype(I32) for n in ("rep", "z", "x", "core")]
    x, *pieces = lax.optimization_barrier((x, *spread_rows(rep[None], amps)))
    half = lax.dynamic_slice_in_dim(integrals, core * HALF, HALF, 0)
    table = product_table(x[None], a_index, b_index, live, owner, target)
    parts = [pieces[0]] + [shift_by(pieces[s], "rep", N_REP, s) for s in range(1, N_REP)]
    half, table = lax.optimization_barrier((half, table))
    lefts, rights = gather(join_k(table, parts), half)
    me = jnp.stack([z, core])
    sums = products(me, sort_products(me, lefts), lefts, [integrals] + rights)
    total = None
    for shift in (2, 1, 3, 0):
        part = sums[N_X + shift].astype(F32) + other_core(sums[shift]).astype(F32)
        if shift > 0:
            part = shift_by(part.astype(BF16), "x", N_X, shift).astype(F32)
        total = part if total is None else total + part
    return total


def solution(mesh):
    devices = mesh.devices.reshape(N_REP, N_Z, N_X, N_CORE)
    fine = Mesh(devices, ("rep", "z", "x", "core"))
    task = ("z", "x", "core")
    in_specs = (
        P(task, None, "rep"),
        P(None, "rep", None),
        P(task),
        P(task),
        P(task),
        P(task, None),
        P(task),
    )
    return jax.shard_map(
        body, mesh=fine, in_specs=in_specs, out_specs=P(task, "rep", None), check_vma=False
    )
```

```python
import jax
import jax.numpy as jnp
from jax import lax
from jax.experimental import pallas as pl
from jax.experimental.pallas import tpu as pltpu
from jax.sharding import Mesh
from jax.sharding import PartitionSpec as P

N_REP, N_Z, N_X, N_CORE = 4, 8, 4, 2
N_SRC = N_Z
A_DEV = 8
OWN_DEV = 8
TPS = 8
NB = 64
HALF = NB // 2
PART = HALF // 2
QUARTER = 64
TILE = 256
MOST = 128
LABELS = 2 * N_Z
SPOTS = N_X * OWN_DEV
GROUP = 4
WIDE = 16
LIST = 1280
NOWHERE = 2.0 * SPOTS * 4096
SORT_COST = 20 * 10**9
ROWS = A_DEV * QUARTER
BLOCK = ROWS + LABELS
JOIN_COST = 20 * 10**9
TABLE_COST = 8 * 10**9
VMEM_LIMIT = 52 * 1024 * 1024
BF16 = jnp.bfloat16
F32 = jnp.float32
I32 = jnp.int32
VMEM = pl.BlockSpec(memory_space=pltpu.VMEM)
SMEM = pl.BlockSpec(memory_space=pltpu.SMEM)
ANY = pl.BlockSpec(memory_space=pl.ANY)


def table_kernel(x_ref, a_ref, b_ref, live_ref, owner_ref, target_ref, out_ref, lines):
    products, slots = a_ref.shape[0], owner_ref.shape[0]
    x = x_ref[0]
    row = lax.broadcasted_iota(I32, (8, slots), 0)
    named = jnp.where(row == 0, owner_ref[...][None], jnp.where(row == 1, target_ref[...][None], 0))
    slot = lax.broadcasted_iota(I32, (slots, products), 0)
    spread = lax.broadcasted_iota(I32, (slots, products), 1) // TPS == slot
    named = jnp.dot(named.astype(F32), spread.astype(F32), precision=lax.Precision.HIGHEST)
    own, target = named[0:1].astype(I32), named[1:2].astype(I32)
    a, b = a_ref[...][None], b_ref[...][None]
    place = jnp.where(live_ref[...][None] > 0, own // (N_X * N_CORE), -1)
    spot = own % N_CORE * SPOTS + ((own // N_CORE - x) & (N_X - 1)) * OWN_DEV + target + 1
    row = lax.broadcasted_iota(I32, (8, products), 0)
    turned = jnp.where(row == 0, place, b).astype(F32).T
    same = turned[:, 0:1] == place.astype(F32)
    order = lax.broadcasted_iota(I32, (products, products), 0)
    same = same & (order < lax.broadcasted_iota(I32, (products, products), 1))
    alike = same & (turned[:, 1:2] == b.astype(F32))
    standing = jnp.sum(same.astype(F32), axis=0, keepdims=True).astype(I32)
    rank = jnp.sum(alike.astype(F32), axis=0, keepdims=True).astype(I32)
    at = jnp.where(place >= 0, place * MOST + standing, -1)
    fields = jnp.where(row == 0, spot, jnp.where(row == 1, a, jnp.where(row == 2, b, rank)))
    fields = fields.astype(F32).astype(BF16)
    position = lax.broadcasted_iota(I32, (MOST, products), 0)
    for place in range(N_Z):
        chosen = (at == position + place * MOST).astype(F32).astype(BF16)
        found = lax.dot_general(
            fields, chosen, (((1,), (1,)), ((), ())), preferred_element_type=F32
        )
        lines[2 * place : 2 * place + 1, :MOST] = found[0:1]
        lines[2 * place : 2 * place + 1, MOST:] = found[1:2]
        lines[2 * place + 1 : 2 * place + 2, :MOST] = found[2:3]
        lines[2 * place + 1 : 2 * place + 2, MOST:] = found[3:4]
    out_ref[...] = lines[...].astype(BF16)


def product_table(x, a_index, b_index, live, owner, target):
    lists = [a_index, b_index, live, owner[:, 0], target]
    return pl.pallas_call(
        table_kernel,
        out_shape=jax.ShapeDtypeStruct((LABELS, 2 * MOST), BF16),
        in_specs=[SMEM] + [VMEM] * 5,
        out_specs=VMEM,
        scratch_shapes=[pltpu.VMEM((LABELS, 2 * MOST), F32)],
        cost_estimate=pl.CostEstimate(flops=TABLE_COST, bytes_accessed=1 << 16, transcendentals=0),
        name="product_table",
    )(x, *lists)


def spread_kernel(rep_ref, left_ref, *refs):
    outs, turned = refs[:N_REP], refs[N_REP]
    for pair in range(4):
        tile = left_ref[2 * pair : 2 * pair + 2].reshape(2 * QUARTER, TILE)
        turned[pair] = tile.T
    for shift in range(N_REP):
        to = lax.rem(rep_ref[0] + shift, N_REP)
        first = pl.multiple_of(to * QUARTER, QUARTER)
        for pair in range(4):
            outs[shift][pair] = turned[pair, pl.ds(first, QUARTER), :]


def spread_rows(rep, left):
    return pl.pallas_call(
        spread_kernel,
        out_shape=[jax.ShapeDtypeStruct((4, QUARTER, 2 * QUARTER), BF16)] * N_REP,
        in_specs=[SMEM, VMEM],
        out_specs=[VMEM] * N_REP,
        scratch_shapes=[pltpu.VMEM((4, TILE, 2 * QUARTER), BF16)],
        name="spread_rows",
    )(rep, left.transpose(0, 2, 1))


def join_kernel(table_ref, *refs):
    parts, out_ref = refs[:N_REP], refs[N_REP]
    for pair in range(4):
        pieces = [part[pair] for part in parts]
        for side in range(2):
            first = (2 * pair + side) * QUARTER
            out_ref[first : first + QUARTER] = jnp.concatenate(
                [p[:, QUARTER * side : QUARTER * (side + 1)] for p in pieces], axis=1
            )
    out_ref[ROWS:BLOCK] = table_ref[...]


def join_k(table, parts):
    return pl.pallas_call(
        join_kernel,
        out_shape=jax.ShapeDtypeStruct((BLOCK, TILE), BF16),
        in_specs=[VMEM] * (N_REP + 1),
        out_specs=VMEM,
        cost_estimate=pl.CostEstimate(flops=JOIN_COST, bytes_accessed=1 << 19, transcendentals=0),
        name="join_k",
    )(table, *parts)


def exact_dot(left, right):
    return jnp.dot(left.astype(F32).astype(BF16), right, preferred_element_type=F32)


def sort_kernel(me_ref, *refs):
    lefts, listed, fetched, labels, sems = refs[:N_SRC], *refs[N_SRC:]
    me = me_ref[0]
    tables = [
        pltpu.make_async_copy(lefts[i].at[pl.ds(ROWS, LABELS)], fetched.at[i], sems.at[i])
        for i in range(N_SRC)
    ]
    for copy in tables:
        copy.start()
    for copy in tables:
        copy.wait()
    labels[...] = fetched[...].astype(F32)
    rows = [labels[i, pl.ds(2 * me + half, 1), :] for half in range(2) for i in range(N_SRC)]
    first = jnp.concatenate(rows[:N_SRC], axis=0)
    second = jnp.concatenate(rows[N_SRC:], axis=0)
    spot, a, b, rank = first[:, :MOST], first[:, MOST:], second[:, :MOST], second[:, MOST:]
    b += (me_ref[1] * HALF).astype(F32)
    b = jnp.where(b < NB, b, b - NB)
    lane = lax.broadcasted_iota(I32, (MOST, MOST), 1)
    row = lax.broadcasted_iota(I32, (MOST, MOST), 0)
    lane_f = lane.astype(F32)
    tile = jnp.where(spot > 0.0, b, float(NB)).T
    rank = rank.T
    of_tile = [(tile[:, i : i + 1] == lane_f).astype(F32).astype(BF16) for i in range(N_SRC)]
    ones = jnp.ones((N_SRC, MOST), F32)
    source = lax.broadcasted_iota(I32, (N_SRC, MOST), 0)
    sizes = jnp.zeros((N_SRC, MOST), F32)
    for i in range(N_SRC):
        sizes = jnp.where(source == i, exact_dot(ones, of_tile[i]), sizes)
    before, below = jnp.zeros((N_SRC, MOST), F32), jnp.zeros((1, MOST), F32)
    for i in range(N_SRC):
        before = jnp.where(source == i, below, before)
        below = below + sizes[i : i + 1]
    groups = jnp.floor((below + (GROUP - 1)) * (1.0 / GROUP))
    groups = jnp.where(lane[:1] < NB, groups, 0.0)
    high = jnp.floor(groups * (1.0 / 128.0))
    earlier = (row < lane).astype(F32).astype(BF16)
    starts = exact_dot(jnp.broadcast_to(groups - 128.0 * high, (N_SRC, MOST)), earlier)
    starts += 128.0 * exact_dot(jnp.broadcast_to(high, (N_SRC, MOST)), earlier)
    starts = GROUP * starts
    base = jnp.where(lane[:N_SRC] < NB, before + starts, 2.0 * LIST)
    high = jnp.floor(base * (1.0 / 128.0))
    low, high = (base - 128.0 * high).T, high.T
    places, fields = [], []
    for i in range(N_SRC):
        place = 128.0 * jnp.dot(of_tile[i], high.astype(BF16), preferred_element_type=F32)
        place += jnp.dot(of_tile[i], low.astype(BF16), preferred_element_type=F32)
        places.append(place[:, i : i + 1] + rank[:, i : i + 1])
        field = jnp.where(source == 0, spot[i : i + 1] - 1.0, a[i : i + 1] + 8.0 * i)
        field = jnp.where(source == 2, b[i : i + 1], field)
        fields.append(jnp.where(source == 3, 1.0, field).astype(BF16))
    field = jnp.concatenate(fields, axis=1)

    def fill(line):
        here = [(place == lane_f + float(line * MOST)).astype(F32).astype(BF16) for place in places]
        found = jnp.dot(field, jnp.concatenate(here, axis=0), preferred_element_type=F32)
        code = found[0:1] * 4096.0 + found[1:2] * 64.0 + found[2:3]
        code = jnp.where(found[3:4] > 0.0, code, NOWHERE)
        listed[line : line + 1, :] = code.astype(I32)

    for line in range(LIST // MOST // 2):
        fill(line)

    @pl.when(jnp.max(starts) > LIST // 2)
    def _():
        for line in range(LIST // MOST // 2, LIST // MOST):
            fill(line)

    listed[LIST // MOST : LIST // MOST + 1, :] = starts[:1].astype(I32)


def sort_products(me, lefts):
    return pl.pallas_call(
        sort_kernel,
        out_shape=jax.ShapeDtypeStruct((LIST // MOST + 1, MOST), I32),
        in_specs=[SMEM] + [ANY] * N_SRC,
        out_specs=VMEM,
        scratch_shapes=[
            pltpu.VMEM((N_SRC, LABELS, TILE), BF16),
            pltpu.VMEM((N_SRC, LABELS, TILE), F32),
            pltpu.SemaphoreType.DMA((N_SRC,)),
        ],
        cost_estimate=pl.CostEstimate(flops=SORT_COST, bytes_accessed=1 << 16, transcendentals=0),
        name="sort_products",
    )(me, *lefts)


STEPS = NB // PART
N_RIGHT = 9


def products_kernel(me_ref, listed, *refs):
    lefts, rights, refs = refs[:N_SRC], refs[N_SRC : N_SRC + N_RIGHT], refs[N_SRC + N_RIGHT :]
    away_refs, home_refs, refs = refs[:N_X], refs[N_X : 2 * N_X], refs[2 * N_X :]
    left, right, total, left_sems, right_sems = refs
    core = me_ref[1]
    copies = [
        pltpu.make_async_copy(lefts[i].at[pl.ds(0, ROWS)], left.at[i], left_sems.at[i])
        for i in range(N_SRC)
    ]
    fetches = []
    for step in range(STEPS):
        first = (core * HALF + step * PART) & (NB - 1)
        back, far_back, far_ahead, ahead = rights[1 + step // 2 * 4 : 5 + step // 2 * 4]
        side = pl.ds(step % 2 * PART, PART)
        sources = [
            rights[0].at[pl.ds(pl.multiple_of(first, PART), PART)],
            back.at[side],
            far_ahead if step % 2 else far_back,
            ahead.at[side],
        ]
        fetches.append(
            [
                pltpu.make_async_copy(
                    source, right.at[q, pl.ds(step * PART, PART)], right_sems.at[4 * step + q]
                )
                for q, source in enumerate(sources)
            ]
        )
    for copy in copies + fetches[0]:
        copy.start()
    total[...] = jnp.zeros_like(total)
    for copy in copies:
        copy.wait()
    for fetch in fetches[1]:
        fetch.start()

    def step(i, carry):
        sums = []
        for w in range(WIDE):
            spots, rows = [], []
            for u in range(GROUP):
                at = (i % 2) * GROUP * WIDE + w * GROUP + u
                code = listed[i // 2, at]
                first = pl.multiple_of(((code >> 6) & 7) * QUARTER, QUARTER)
                rows.append(left[(code >> 9) & 7, pl.ds(first, QUARTER), :])
                spots.append(code >> 12)
                b = code & (NB - 1) if u == 0 else b
            tile = jnp.concatenate([right[q, b] for q in range(N_REP)], axis=0)
            lhs = jnp.concatenate(rows, axis=0)
            sums.append((spots, jnp.dot(lhs, tile, preferred_element_type=F32)))
        for spots, value in sums:
            for u in range(GROUP):
                total[spots[u]] += value[u * QUARTER : (u + 1) * QUARTER]
        return carry

    done = 0
    for part in range(STEPS):
        for fetch in fetches[part]:
            fetch.wait()
        if part + 2 < STEPS:
            for fetch in fetches[part + 2]:
                fetch.start()
        end = listed[LIST // MOST, (part + 1) * PART]
        end = end // (GROUP * WIDE) if part < STEPS - 1 else (end + GROUP * WIDE - 1) // (GROUP * WIDE)
        lax.fori_loop(done, end, step, 0)
        done = end
    for refs, owner_core in ((away_refs, 1 - core), (home_refs, core)):
        for shift, ref in enumerate(refs):
            first = pl.multiple_of(owner_core * SPOTS + shift * OWN_DEV, OWN_DEV)
            ref[...] = total[pl.ds(first, OWN_DEV)].astype(ref.dtype)


def products(me, listed, lefts, rights):
    shape = (OWN_DEV, QUARTER, TILE)
    types = [BF16] * N_X + [F32] + [BF16] * (N_X - 1)
    return pl.pallas_call(
        products_kernel,
        out_shape=[jax.ShapeDtypeStruct(shape, kind) for kind in types],
        in_specs=[SMEM] * 2 + [ANY] * (N_SRC + N_RIGHT),
        out_specs=[VMEM] * (2 * N_X),
        scratch_shapes=[
            pltpu.VMEM((N_SRC, ROWS, TILE), BF16),
            pltpu.VMEM((N_REP, NB, QUARTER, TILE), BF16),
            pltpu.VMEM((2 * SPOTS + 1, QUARTER, TILE), F32),
            pltpu.SemaphoreType.DMA((N_SRC,)),
            pltpu.SemaphoreType.DMA((N_REP * STEPS,)),
        ],
        compiler_params=pltpu.CompilerParams(vmem_limit_bytes=VMEM_LIMIT),
        cost_estimate=pl.CostEstimate(
            flops=2 * 384 * 64 * 256 * 256, bytes_accessed=10 << 20, transcendentals=0
        ),
        name="products",
    )(me, listed, *lefts, *rights)


def shift_by(value, axis, size, step):
    return lax.ppermute(value, axis, [(i, (i + step) % size) for i in range(size)])


def apart(value, axis, size):
    perm = []
    for i in range(size):
        perm.append((i * 2, ((i + 1) % size) * 2))
        perm.append((i * 2 + 1, ((i - 1) % size) * 2 + 1))
    return lax.ppermute(value, (axis, "core"), perm)


def other_core(value):
    return lax.ppermute(value, "core", [(0, 1), (1, 0)])


def gather(mine, half):
    back = shift_by(half, "rep", N_REP, 1)
    ahead = shift_by(half, "rep", N_REP, -1)
    own, other = mine, other_core(mine)
    blocks = [own]
    for distance in range(3):
        own, other = apart(own, "z", N_Z), apart(other, "z", N_Z)
        blocks += [own, other]
    far_back = shift_by(back[: HALF // 2], "rep", N_REP, 1)
    far_ahead = shift_by(ahead[HALF // 2 :], "rep", N_REP, -1)
    parts = [back, far_back, far_ahead, ahead]
    return blocks + [apart(own, "z", N_Z)], parts + [other_core(part) for part in parts]


def body(amps, integrals, a_index, b_index, live, owner, target):
    rep, z, x, core = [lax.axis_index(n).astype(I32) for n in ("rep", "z", "x", "core")]
    x, *pieces = lax.optimization_barrier((x, *spread_rows(rep[None], amps)))
    half = lax.dynamic_slice_in_dim(integrals, core * HALF, HALF, 0)
    table = product_table(x[None], a_index, b_index, live, owner, target)
    parts = [pieces[0]] + [shift_by(pieces[s], "rep", N_REP, s) for s in range(1, N_REP)]
    half, table = lax.optimization_barrier((half, table))
    lefts, rights = gather(join_k(table, parts), half)
    me = jnp.stack([z, core])
    sums = products(me, sort_products(me, lefts), lefts, [integrals] + rights)
    total = None
    for shift in (2, 1, 3, 0):
        part = sums[N_X + shift].astype(F32) + other_core(sums[shift]).astype(F32)
        if shift > 0:
            part = shift_by(part.astype(BF16), "x", N_X, shift).astype(F32)
        total = part if total is None else total + part
    return total


def solution(mesh):
    devices = mesh.devices.reshape(N_REP, N_Z, N_X, N_CORE)
    fine = Mesh(devices, ("rep", "z", "x", "core"))
    task = ("z", "x", "core")
    in_specs = (
        P(task, None, "rep"),
        P(None, "rep", None),
        P(task),
        P(task),
        P(task),
        P(task, None),
        P(task),
    )
    return jax.shard_map(
        body, mesh=fine, in_specs=in_specs, out_specs=P(task, "rep", None), check_vma=False
    )
```

```python
import jax
import jax.numpy as jnp
from jax import lax
from jax.experimental import pallas as pl
from jax.experimental.pallas import tpu as pltpu
from jax.sharding import Mesh
from jax.sharding import PartitionSpec as P

N_REP, N_Z, N_X, N_CORE = 4, 8, 4, 2
N_SRC = N_Z
A_DEV = 8
OWN_DEV = 8
TPS = 8
NB = 64
HALF = NB // 2
PART = HALF // 2
QUARTER = 64
TILE = 256
MOST = 128
LABELS = 2 * N_Z
SPOTS = N_X * OWN_DEV
GROUP = 4
WIDE = 16
LIST = 1280
NOWHERE = 2.0 * SPOTS * 4096
SORT_COST = 20 * 10**9
ROWS = A_DEV * QUARTER
BLOCK = ROWS + LABELS
JOIN_COST = 20 * 10**9
TABLE_COST = 8 * 10**9
VMEM_LIMIT = 52 * 1024 * 1024
BF16 = jnp.bfloat16
F32 = jnp.float32
I32 = jnp.int32
VMEM = pl.BlockSpec(memory_space=pltpu.VMEM)
SMEM = pl.BlockSpec(memory_space=pltpu.SMEM)
ANY = pl.BlockSpec(memory_space=pl.ANY)


def table_kernel(x_ref, a_ref, b_ref, live_ref, owner_ref, target_ref, out_ref, lines):
    products, slots = a_ref.shape[0], owner_ref.shape[0]
    x = x_ref[0]
    row = lax.broadcasted_iota(I32, (8, slots), 0)
    named = jnp.where(row == 0, owner_ref[...][None], jnp.where(row == 1, target_ref[...][None], 0))
    slot = lax.broadcasted_iota(I32, (slots, products), 0)
    spread = lax.broadcasted_iota(I32, (slots, products), 1) // TPS == slot
    named = jnp.dot(named.astype(F32), spread.astype(F32), precision=lax.Precision.HIGHEST)
    own, target = named[0:1].astype(I32), named[1:2].astype(I32)
    a, b = a_ref[...][None], b_ref[...][None]
    place = jnp.where(live_ref[...][None] > 0, own // (N_X * N_CORE), -1)
    spot = own % N_CORE * SPOTS + ((own // N_CORE - x) & (N_X - 1)) * OWN_DEV + target + 1
    row = lax.broadcasted_iota(I32, (8, products), 0)
    turned = jnp.where(row == 0, place, b).astype(F32).T
    same = turned[:, 0:1] == place.astype(F32)
    order = lax.broadcasted_iota(I32, (products, products), 0)
    same = same & (order < lax.broadcasted_iota(I32, (products, products), 1))
    alike = same & (turned[:, 1:2] == b.astype(F32))
    standing = jnp.sum(same.astype(F32), axis=0, keepdims=True).astype(I32)
    rank = jnp.sum(alike.astype(F32), axis=0, keepdims=True).astype(I32)
    at = jnp.where(place >= 0, place * MOST + standing, -1)
    fields = jnp.where(row == 0, spot, jnp.where(row == 1, a, jnp.where(row == 2, b, rank)))
    fields = fields.astype(F32).astype(BF16)
    position = lax.broadcasted_iota(I32, (MOST, products), 0)
    for place in range(N_Z):
        chosen = (at == position + place * MOST).astype(F32).astype(BF16)
        found = lax.dot_general(
            fields, chosen, (((1,), (1,)), ((), ())), preferred_element_type=F32
        )
        lines[2 * place : 2 * place + 1, :MOST] = found[0:1]
        lines[2 * place : 2 * place + 1, MOST:] = found[1:2]
        lines[2 * place + 1 : 2 * place + 2, :MOST] = found[2:3]
        lines[2 * place + 1 : 2 * place + 2, MOST:] = found[3:4]
    out_ref[...] = lines[...].astype(BF16)


def product_table(x, a_index, b_index, live, owner, target):
    lists = [a_index, b_index, live, owner[:, 0], target]
    return pl.pallas_call(
        table_kernel,
        out_shape=jax.ShapeDtypeStruct((LABELS, 2 * MOST), BF16),
        in_specs=[SMEM] + [VMEM] * 5,
        out_specs=VMEM,
        scratch_shapes=[pltpu.VMEM((LABELS, 2 * MOST), F32)],
        cost_estimate=pl.CostEstimate(flops=TABLE_COST, bytes_accessed=1 << 16, transcendentals=0),
        name="product_table",
    )(x, *lists)


def spread_kernel(rep_ref, left_ref, *refs):
    outs, turned = refs[:N_REP], refs[N_REP]
    for pair in range(4):
        tile = left_ref[2 * pair : 2 * pair + 2].reshape(2 * QUARTER, TILE)
        turned[pair] = tile.T
    for shift in range(N_REP):
        to = lax.rem(rep_ref[0] + shift, N_REP)
        first = pl.multiple_of(to * QUARTER, QUARTER)
        for pair in range(4):
            outs[shift][pair] = turned[pair, pl.ds(first, QUARTER), :]


def spread_rows(rep, left):
    return pl.pallas_call(
        spread_kernel,
        out_shape=[jax.ShapeDtypeStruct((4, QUARTER, 2 * QUARTER), BF16)] * N_REP,
        in_specs=[SMEM, VMEM],
        out_specs=[VMEM] * N_REP,
        scratch_shapes=[pltpu.VMEM((4, TILE, 2 * QUARTER), BF16)],
        name="spread_rows",
    )(rep, left.transpose(0, 2, 1))


def join_kernel(table_ref, *refs):
    parts, out_ref = refs[:N_REP], refs[N_REP]
    for pair in range(4):
        pieces = [part[pair] for part in parts]
        for side in range(2):
            first = (2 * pair + side) * QUARTER
            out_ref[first : first + QUARTER] = jnp.concatenate(
                [p[:, QUARTER * side : QUARTER * (side + 1)] for p in pieces], axis=1
            )
    out_ref[ROWS:BLOCK] = table_ref[...]


def join_k(table, parts):
    return pl.pallas_call(
        join_kernel,
        out_shape=jax.ShapeDtypeStruct((BLOCK, TILE), BF16),
        in_specs=[VMEM] * (N_REP + 1),
        out_specs=VMEM,
        cost_estimate=pl.CostEstimate(flops=JOIN_COST, bytes_accessed=1 << 19, transcendentals=0),
        name="join_k",
    )(table, *parts)


def exact_dot(left, right):
    return jnp.dot(left.astype(F32).astype(BF16), right, preferred_element_type=F32)


def sort_kernel(me_ref, *refs):
    lefts, listed, fetched, labels, sems = refs[:N_SRC], *refs[N_SRC:]
    me = me_ref[0]
    tables = [
        pltpu.make_async_copy(lefts[i].at[pl.ds(ROWS, LABELS)], fetched.at[i], sems.at[i])
        for i in range(N_SRC)
    ]
    for copy in tables:
        copy.start()
    for copy in tables:
        copy.wait()
    labels[...] = fetched[...].astype(F32)
    rows = [labels[i, pl.ds(2 * me + half, 1), :] for half in range(2) for i in range(N_SRC)]
    first = jnp.concatenate(rows[:N_SRC], axis=0)
    second = jnp.concatenate(rows[N_SRC:], axis=0)
    spot, a, b, rank = first[:, :MOST], first[:, MOST:], second[:, :MOST], second[:, MOST:]
    b += (me_ref[1] * HALF).astype(F32)
    b = jnp.where(b < NB, b, b - NB)
    lane = lax.broadcasted_iota(I32, (MOST, MOST), 1)
    row = lax.broadcasted_iota(I32, (MOST, MOST), 0)
    lane_f = lane.astype(F32)
    tile = jnp.where(spot > 0.0, b, float(NB)).T
    rank = rank.T
    of_tile = [(tile[:, i : i + 1] == lane_f).astype(F32).astype(BF16) for i in range(N_SRC)]
    ones = jnp.ones((N_SRC, MOST), F32)
    source = lax.broadcasted_iota(I32, (N_SRC, MOST), 0)
    sizes = jnp.zeros((N_SRC, MOST), F32)
    for i in range(N_SRC):
        sizes = jnp.where(source == i, exact_dot(ones, of_tile[i]), sizes)
    before, below = jnp.zeros((N_SRC, MOST), F32), jnp.zeros((1, MOST), F32)
    for i in range(N_SRC):
        before = jnp.where(source == i, below, before)
        below = below + sizes[i : i + 1]
    groups = jnp.floor((below + (GROUP - 1)) * (1.0 / GROUP))
    groups = jnp.where(lane[:1] < NB, groups, 0.0)
    high = jnp.floor(groups * (1.0 / 128.0))
    earlier = (row < lane).astype(F32).astype(BF16)
    starts = exact_dot(jnp.broadcast_to(groups - 128.0 * high, (N_SRC, MOST)), earlier)
    starts += 128.0 * exact_dot(jnp.broadcast_to(high, (N_SRC, MOST)), earlier)
    starts = GROUP * starts
    base = jnp.where(lane[:N_SRC] < NB, before + starts, 2.0 * LIST)
    high = jnp.floor(base * (1.0 / 128.0))
    low, high = (base - 128.0 * high).T, high.T
    places, fields = [], []
    for i in range(N_SRC):
        place = 128.0 * jnp.dot(of_tile[i], high.astype(BF16), preferred_element_type=F32)
        place += jnp.dot(of_tile[i], low.astype(BF16), preferred_element_type=F32)
        places.append(place[:, i : i + 1] + rank[:, i : i + 1])
        field = jnp.where(source == 0, spot[i : i + 1] - 1.0, a[i : i + 1] + 8.0 * i)
        field = jnp.where(source == 2, b[i : i + 1], field)
        fields.append(jnp.where(source == 3, 1.0, field).astype(BF16))
    field = jnp.concatenate(fields, axis=1)

    def fill(line):
        here = [(place == lane_f + float(line * MOST)).astype(F32).astype(BF16) for place in places]
        found = jnp.dot(field, jnp.concatenate(here, axis=0), preferred_element_type=F32)
        code = found[0:1] * 4096.0 + found[1:2] * 64.0 + found[2:3]
        code = jnp.where(found[3:4] > 0.0, code, NOWHERE)
        listed[line : line + 1, :] = code.astype(I32)

    for line in range(LIST // MOST // 2):
        fill(line)

    @pl.when(jnp.max(starts) > LIST // 2)
    def _():
        for line in range(LIST // MOST // 2, LIST // MOST):
            fill(line)

    listed[LIST // MOST : LIST // MOST + 1, :] = starts[:1].astype(I32)


def sort_products(me, lefts):
    return pl.pallas_call(
        sort_kernel,
        out_shape=jax.ShapeDtypeStruct((LIST // MOST + 1, MOST), I32),
        in_specs=[SMEM] + [ANY] * N_SRC,
        out_specs=VMEM,
        scratch_shapes=[
            pltpu.VMEM((N_SRC, LABELS, TILE), BF16),
            pltpu.VMEM((N_SRC, LABELS, TILE), F32),
            pltpu.SemaphoreType.DMA((N_SRC,)),
        ],
        cost_estimate=pl.CostEstimate(flops=SORT_COST, bytes_accessed=1 << 16, transcendentals=0),
        name="sort_products",
    )(me, *lefts)


STEPS = NB // PART
N_RIGHT = 9


def products_kernel(me_ref, listed, *refs):
    lefts, rights, refs = refs[:N_SRC], refs[N_SRC : N_SRC + N_RIGHT], refs[N_SRC + N_RIGHT :]
    away_refs, home_refs, refs = refs[:N_X], refs[N_X : 2 * N_X], refs[2 * N_X :]
    left, right, total, left_sems, right_sems = refs
    core = me_ref[1]
    copies = [
        pltpu.make_async_copy(lefts[i].at[pl.ds(0, ROWS)], left.at[i], left_sems.at[i])
        for i in range(N_SRC)
    ]
    fetches = []
    for step in range(STEPS):
        first = (core * HALF + step * PART) & (NB - 1)
        back, far_back, far_ahead, ahead = rights[1 + step // 2 * 4 : 5 + step // 2 * 4]
        side = pl.ds(step % 2 * PART, PART)
        sources = [
            rights[0].at[pl.ds(pl.multiple_of(first, PART), PART)],
            back.at[side],
            far_ahead if step % 2 else far_back,
            ahead.at[side],
        ]
        fetches.append(
            [
                pltpu.make_async_copy(
                    source, right.at[q, pl.ds(step * PART, PART)], right_sems.at[4 * step + q]
                )
                for q, source in enumerate(sources)
            ]
        )
    for copy in copies + fetches[0]:
        copy.start()
    total[...] = jnp.zeros_like(total)
    for copy in copies:
        copy.wait()
    for fetch in fetches[1]:
        fetch.start()

    def step(i, carry):
        sums = []
        for w in range(WIDE):
            spots, rows = [], []
            for u in range(GROUP):
                at = (i % 2) * GROUP * WIDE + w * GROUP + u
                code = listed[i // 2, at]
                first = pl.multiple_of(((code >> 6) & 7) * QUARTER, QUARTER)
                rows.append(left[(code >> 9) & 7, pl.ds(first, QUARTER), :])
                spots.append(code >> 12)
                b = code & (NB - 1) if u == 0 else b
            tile = jnp.concatenate([right[q, b] for q in range(N_REP)], axis=0)
            lhs = jnp.concatenate(rows, axis=0)
            sums.append((spots, jnp.dot(lhs, tile, preferred_element_type=F32)))
        for spots, value in sums:
            for u in range(GROUP):
                total[spots[u]] += value[u * QUARTER : (u + 1) * QUARTER]
        return carry

    done = 0
    for part in range(STEPS):
        for fetch in fetches[part]:
            fetch.wait()
        if part + 2 < STEPS:
            for fetch in fetches[part + 2]:
                fetch.start()
        end = listed[LIST // MOST, (part + 1) * PART]
        end = end // (GROUP * WIDE) if part < STEPS - 1 else (end + GROUP * WIDE - 1) // (GROUP * WIDE)
        lax.fori_loop(done, end, step, 0)
        done = end
    for refs, owner_core in ((away_refs, 1 - core), (home_refs, core)):
        for shift, ref in enumerate(refs):
            first = pl.multiple_of(owner_core * SPOTS + shift * OWN_DEV, OWN_DEV)
            ref[...] = total[pl.ds(first, OWN_DEV)].astype(ref.dtype)


def products(me, listed, lefts, rights):
    shape = (OWN_DEV, QUARTER, TILE)
    types = [BF16] * N_X + [F32] + [BF16] * (N_X - 1)
    return pl.pallas_call(
        products_kernel,
        out_shape=[jax.ShapeDtypeStruct(shape, kind) for kind in types],
        in_specs=[SMEM] * 2 + [ANY] * (N_SRC + N_RIGHT),
        out_specs=[VMEM] * (2 * N_X),
        scratch_shapes=[
            pltpu.VMEM((N_SRC, ROWS, TILE), BF16),
            pltpu.VMEM((N_REP, NB, QUARTER, TILE), BF16),
            pltpu.VMEM((2 * SPOTS + 1, QUARTER, TILE), F32),
            pltpu.SemaphoreType.DMA((N_SRC,)),
            pltpu.SemaphoreType.DMA((N_REP * STEPS,)),
        ],
        compiler_params=pltpu.CompilerParams(vmem_limit_bytes=VMEM_LIMIT),
        cost_estimate=pl.CostEstimate(
            flops=2 * 384 * 64 * 256 * 256, bytes_accessed=10 << 20, transcendentals=0
        ),
        name="products",
    )(me, listed, *lefts, *rights)


def shift_by(value, axis, size, step):
    return lax.ppermute(value, axis, [(i, (i + step) % size) for i in range(size)])


def apart(value, axis, size):
    perm = []
    for i in range(size):
        perm.append((i * 2, ((i + 1) % size) * 2))
        perm.append((i * 2 + 1, ((i - 1) % size) * 2 + 1))
    return lax.ppermute(value, (axis, "core"), perm)


def other_core(value):
    return lax.ppermute(value, "core", [(0, 1), (1, 0)])


def gather(mine, half):
    back = shift_by(half, "rep", N_REP, 1)
    ahead = shift_by(half, "rep", N_REP, -1)
    own, other = mine, other_core(mine)
    blocks = [own]
    for distance in range(3):
        own, other = apart(own, "z", N_Z), apart(other, "z", N_Z)
        blocks += [own, other]
        if distance == 1:
            back, ahead, _ = lax.optimization_barrier((back, ahead, other))
    far_back = shift_by(back[: HALF // 2], "rep", N_REP, 1)
    far_ahead = shift_by(ahead[HALF // 2 :], "rep", N_REP, -1)
    parts = [back, far_back, far_ahead, ahead]
    return blocks + [apart(own, "z", N_Z)], parts + [other_core(part) for part in parts]


def body(amps, integrals, a_index, b_index, live, owner, target):
    rep, z, x, core = [lax.axis_index(n).astype(I32) for n in ("rep", "z", "x", "core")]
    x, *pieces = lax.optimization_barrier((x, *spread_rows(rep[None], amps)))
    half = lax.dynamic_slice_in_dim(integrals, core * HALF, HALF, 0)
    table = product_table(x[None], a_index, b_index, live, owner, target)
    parts = [pieces[0]] + [shift_by(pieces[s], "rep", N_REP, s) for s in range(1, N_REP)]
    half, table = lax.optimization_barrier((half, table))
    lefts, rights = gather(join_k(table, parts), half)
    me = jnp.stack([z, core])
    sums = products(me, sort_products(me, lefts), lefts, [integrals] + rights)
    total = None
    for shift in (2, 1, 3, 0):
        part = sums[N_X + shift].astype(F32) + other_core(sums[shift]).astype(F32)
        if shift > 0:
            part = shift_by(part.astype(BF16), "x", N_X, shift).astype(F32)
        total = part if total is None else total + part
    return total


def solution(mesh):
    devices = mesh.devices.reshape(N_REP, N_Z, N_X, N_CORE)
    fine = Mesh(devices, ("rep", "z", "x", "core"))
    task = ("z", "x", "core")
    in_specs = (
        P(task, None, "rep"),
        P(None, "rep", None),
        P(task),
        P(task),
        P(task),
        P(task, None),
        P(task),
    )
    return jax.shard_map(
        body, mesh=fine, in_specs=in_specs, out_specs=P(task, "rep", None), check_vma=False
    )
```

```python
import jax
import jax.numpy as jnp
from jax import lax
from jax.experimental import pallas as pl
from jax.experimental.pallas import tpu as pltpu
from jax.sharding import Mesh
from jax.sharding import PartitionSpec as P

N_REP, N_Z, N_X, N_CORE = 4, 8, 4, 2
N_SRC = N_Z
A_DEV = 8
OWN_DEV = 8
TPS = 8
NB = 64
HALF = NB // 2
PART = HALF // 2
QUARTER = 64
TILE = 256
MOST = 128
LABELS = 2 * N_Z
SPOTS = N_X * OWN_DEV
GROUP = 4
WIDE = 16
LIST = 1280
NOWHERE = 2.0 * SPOTS * 4096
SORT_COST = 20 * 10**9
ROWS = A_DEV * QUARTER
BLOCK = ROWS + LABELS
JOIN_COST = 20 * 10**9
TABLE_COST = 8 * 10**9
VMEM_LIMIT = 52 * 1024 * 1024
BF16 = jnp.bfloat16
F32 = jnp.float32
I32 = jnp.int32
VMEM = pl.BlockSpec(memory_space=pltpu.VMEM)
SMEM = pl.BlockSpec(memory_space=pltpu.SMEM)
ANY = pl.BlockSpec(memory_space=pl.ANY)


def table_kernel(x_ref, a_ref, b_ref, live_ref, owner_ref, target_ref, out_ref, lines):
    products, slots = a_ref.shape[0], owner_ref.shape[0]
    x = x_ref[0]
    row = lax.broadcasted_iota(I32, (8, slots), 0)
    named = jnp.where(row == 0, owner_ref[...][None], jnp.where(row == 1, target_ref[...][None], 0))
    slot = lax.broadcasted_iota(I32, (slots, products), 0)
    spread = lax.broadcasted_iota(I32, (slots, products), 1) // TPS == slot
    named = exact_dot(named, spread.astype(F32).astype(BF16))
    own, target = named[0:1].astype(I32), named[1:2].astype(I32)
    a, b = a_ref[...][None], b_ref[...][None]
    place = jnp.where(live_ref[...][None] > 0, own // (N_X * N_CORE), -1)
    spot = own % N_CORE * SPOTS + ((own // N_CORE - x) & (N_X - 1)) * OWN_DEV + target + 1
    row = lax.broadcasted_iota(I32, (8, products), 0)
    turned = jnp.where(row == 0, place, b).astype(F32).T
    same = turned[:, 0:1] == place.astype(F32)
    order = lax.broadcasted_iota(I32, (products, products), 0)
    same = same & (order < lax.broadcasted_iota(I32, (products, products), 1))
    alike = same & (turned[:, 1:2] == b.astype(F32))
    standing = jnp.sum(same.astype(F32), axis=0, keepdims=True).astype(I32)
    rank = jnp.sum(alike.astype(F32), axis=0, keepdims=True).astype(I32)
    at = jnp.where(place >= 0, place * MOST + standing, -1)
    fields = jnp.where(row == 0, spot, jnp.where(row == 1, a, jnp.where(row == 2, b, rank)))
    fields = fields.astype(F32).astype(BF16)
    position = lax.broadcasted_iota(I32, (MOST, products), 0)
    for place in range(N_Z):
        chosen = (at == position + place * MOST).astype(F32).astype(BF16)
        found = lax.dot_general(
            fields, chosen, (((1,), (1,)), ((), ())), preferred_element_type=F32
        )
        lines[2 * place : 2 * place + 1, :MOST] = found[0:1]
        lines[2 * place : 2 * place + 1, MOST:] = found[1:2]
        lines[2 * place + 1 : 2 * place + 2, :MOST] = found[2:3]
        lines[2 * place + 1 : 2 * place + 2, MOST:] = found[3:4]
    out_ref[...] = lines[...].astype(BF16)


def product_table(x, a_index, b_index, live, owner, target):
    lists = [a_index, b_index, live, owner[:, 0], target]
    return pl.pallas_call(
        table_kernel,
        out_shape=jax.ShapeDtypeStruct((LABELS, 2 * MOST), BF16),
        in_specs=[SMEM] + [VMEM] * 5,
        out_specs=VMEM,
        scratch_shapes=[pltpu.VMEM((LABELS, 2 * MOST), F32)],
        cost_estimate=pl.CostEstimate(flops=TABLE_COST, bytes_accessed=1 << 16, transcendentals=0),
        name="product_table",
    )(x, *lists)


def spread_kernel(rep_ref, left_ref, *refs):
    outs, turned = refs[:N_REP], refs[N_REP]
    for pair in range(4):
        tile = left_ref[2 * pair : 2 * pair + 2].reshape(2 * QUARTER, TILE)
        turned[pair] = tile.T
    for shift in range(N_REP):
        to = lax.rem(rep_ref[0] + shift, N_REP)
        first = pl.multiple_of(to * QUARTER, QUARTER)
        for pair in range(4):
            outs[shift][pair] = turned[pair, pl.ds(first, QUARTER), :]


def spread_rows(rep, left):
    return pl.pallas_call(
        spread_kernel,
        out_shape=[jax.ShapeDtypeStruct((4, QUARTER, 2 * QUARTER), BF16)] * N_REP,
        in_specs=[SMEM, VMEM],
        out_specs=[VMEM] * N_REP,
        scratch_shapes=[pltpu.VMEM((4, TILE, 2 * QUARTER), BF16)],
        name="spread_rows",
    )(rep, left.transpose(0, 2, 1))


def join_kernel(table_ref, *refs):
    parts, out_ref = refs[:N_REP], refs[N_REP]
    for pair in range(4):
        pieces = [part[pair] for part in parts]
        for side in range(2):
            first = (2 * pair + side) * QUARTER
            out_ref[first : first + QUARTER] = jnp.concatenate(
                [p[:, QUARTER * side : QUARTER * (side + 1)] for p in pieces], axis=1
            )
    out_ref[ROWS:BLOCK] = table_ref[...]


def join_k(table, parts):
    return pl.pallas_call(
        join_kernel,
        out_shape=jax.ShapeDtypeStruct((BLOCK, TILE), BF16),
        in_specs=[VMEM] * (N_REP + 1),
        out_specs=VMEM,
        cost_estimate=pl.CostEstimate(flops=JOIN_COST, bytes_accessed=1 << 19, transcendentals=0),
        name="join_k",
    )(table, *parts)


def exact_dot(left, right):
    return jnp.dot(left.astype(F32).astype(BF16), right, preferred_element_type=F32)


def sort_kernel(me_ref, *refs):
    lefts, listed, fetched, labels, sems = refs[:N_SRC], *refs[N_SRC:]
    me = me_ref[0]
    tables = [
        pltpu.make_async_copy(lefts[i].at[pl.ds(ROWS, LABELS)], fetched.at[i], sems.at[i])
        for i in range(N_SRC)
    ]
    for copy in tables:
        copy.start()
    for copy in tables:
        copy.wait()
    labels[...] = fetched[...].astype(F32)
    rows = [labels[i, pl.ds(2 * me + half, 1), :] for half in range(2) for i in range(N_SRC)]
    first = jnp.concatenate(rows[:N_SRC], axis=0)
    second = jnp.concatenate(rows[N_SRC:], axis=0)
    spot, a, b, rank = first[:, :MOST], first[:, MOST:], second[:, :MOST], second[:, MOST:]
    b += (me_ref[1] * HALF).astype(F32)
    b = jnp.where(b < NB, b, b - NB)
    lane = lax.broadcasted_iota(I32, (MOST, MOST), 1)
    row = lax.broadcasted_iota(I32, (MOST, MOST), 0)
    lane_f = lane.astype(F32)
    tile = jnp.where(spot > 0.0, b, float(NB)).T
    rank = rank.T
    of_tile = [(tile[:, i : i + 1] == lane_f).astype(F32).astype(BF16) for i in range(N_SRC)]
    ones = jnp.ones((N_SRC, MOST), F32)
    source = lax.broadcasted_iota(I32, (N_SRC, MOST), 0)
    sizes = jnp.zeros((N_SRC, MOST), F32)
    for i in range(N_SRC):
        sizes = jnp.where(source == i, exact_dot(ones, of_tile[i]), sizes)
    before, below = jnp.zeros((N_SRC, MOST), F32), jnp.zeros((1, MOST), F32)
    for i in range(N_SRC):
        before = jnp.where(source == i, below, before)
        below = below + sizes[i : i + 1]
    groups = jnp.floor((below + (GROUP - 1)) * (1.0 / GROUP))
    groups = jnp.where(lane[:1] < NB, groups, 0.0)
    high = jnp.floor(groups * (1.0 / 128.0))
    earlier = (row < lane).astype(F32).astype(BF16)
    starts = exact_dot(jnp.broadcast_to(groups - 128.0 * high, (N_SRC, MOST)), earlier)
    starts += 128.0 * exact_dot(jnp.broadcast_to(high, (N_SRC, MOST)), earlier)
    starts = GROUP * starts
    base = jnp.where(lane[:N_SRC] < NB, before + starts, 2.0 * LIST)
    high = jnp.floor(base * (1.0 / 128.0))
    low, high = (base - 128.0 * high).T, high.T
    places, fields = [], []
    for i in range(N_SRC):
        place = 128.0 * jnp.dot(of_tile[i], high.astype(BF16), preferred_element_type=F32)
        place += jnp.dot(of_tile[i], low.astype(BF16), preferred_element_type=F32)
        places.append(place[:, i : i + 1] + rank[:, i : i + 1])
        field = jnp.where(source == 0, spot[i : i + 1] - 1.0, a[i : i + 1] + 8.0 * i)
        field = jnp.where(source == 2, b[i : i + 1], field)
        fields.append(jnp.where(source == 3, 1.0, field).astype(BF16))
    field = jnp.concatenate(fields, axis=1)

    def fill(line):
        here = [(place == lane_f + float(line * MOST)).astype(F32).astype(BF16) for place in places]
        found = jnp.dot(field, jnp.concatenate(here, axis=0), preferred_element_type=F32)
        code = found[0:1] * 4096.0 + found[1:2] * 64.0 + found[2:3]
        code = jnp.where(found[3:4] > 0.0, code, NOWHERE)
        listed[line : line + 1, :] = code.astype(I32)

    for line in range(LIST // MOST // 2):
        fill(line)

    @pl.when(jnp.max(starts) > LIST // 2)
    def _():
        for line in range(LIST // MOST // 2, LIST // MOST):
            fill(line)

    listed[LIST // MOST : LIST // MOST + 1, :] = starts[:1].astype(I32)


def sort_products(me, lefts):
    return pl.pallas_call(
        sort_kernel,
        out_shape=jax.ShapeDtypeStruct((LIST // MOST + 1, MOST), I32),
        in_specs=[SMEM] + [ANY] * N_SRC,
        out_specs=VMEM,
        scratch_shapes=[
            pltpu.VMEM((N_SRC, LABELS, TILE), BF16),
            pltpu.VMEM((N_SRC, LABELS, TILE), F32),
            pltpu.SemaphoreType.DMA((N_SRC,)),
        ],
        cost_estimate=pl.CostEstimate(flops=SORT_COST, bytes_accessed=1 << 16, transcendentals=0),
        name="sort_products",
    )(me, *lefts)


STEPS = NB // PART
N_RIGHT = 9


def products_kernel(me_ref, listed, *refs):
    lefts, rights, refs = refs[:N_SRC], refs[N_SRC : N_SRC + N_RIGHT], refs[N_SRC + N_RIGHT :]
    away_refs, home_refs, refs = refs[:N_X], refs[N_X : 2 * N_X], refs[2 * N_X :]
    left, right, total, left_sems, right_sems = refs
    core = me_ref[1]
    copies = [
        pltpu.make_async_copy(lefts[i].at[pl.ds(0, ROWS)], left.at[i], left_sems.at[i])
        for i in range(N_SRC)
    ]
    fetches = []
    for step in range(STEPS):
        first = (core * HALF + step * PART) & (NB - 1)
        back, far_back, far_ahead, ahead = rights[1 + step // 2 * 4 : 5 + step // 2 * 4]
        side = pl.ds(step % 2 * PART, PART)
        sources = [
            rights[0].at[pl.ds(pl.multiple_of(first, PART), PART)],
            back.at[side],
            far_ahead if step % 2 else far_back,
            ahead.at[side],
        ]
        fetches.append(
            [
                pltpu.make_async_copy(
                    source, right.at[q, pl.ds(step * PART, PART)], right_sems.at[4 * step + q]
                )
                for q, source in enumerate(sources)
            ]
        )
    for copy in copies + fetches[0]:
        copy.start()
    total[...] = jnp.zeros_like(total)
    for copy in copies:
        copy.wait()
    for fetch in fetches[1]:
        fetch.start()

    def step(i, carry):
        sums = []
        for w in range(WIDE):
            spots, rows = [], []
            for u in range(GROUP):
                at = (i % 2) * GROUP * WIDE + w * GROUP + u
                code = listed[i // 2, at]
                first = pl.multiple_of(((code >> 6) & 7) * QUARTER, QUARTER)
                rows.append(left[(code >> 9) & 7, pl.ds(first, QUARTER), :])
                spots.append(code >> 12)
                b = code & (NB - 1) if u == 0 else b
            tile = jnp.concatenate([right[q, b] for q in range(N_REP)], axis=0)
            lhs = jnp.concatenate(rows, axis=0)
            sums.append((spots, jnp.dot(lhs, tile, preferred_element_type=F32)))
        for spots, value in sums:
            for u in range(GROUP):
                total[spots[u]] += value[u * QUARTER : (u + 1) * QUARTER]
        return carry

    done = 0
    for part in range(STEPS):
        for fetch in fetches[part]:
            fetch.wait()
        if part + 2 < STEPS:
            for fetch in fetches[part + 2]:
                fetch.start()
        end = listed[LIST // MOST, (part + 1) * PART]
        end = end // (GROUP * WIDE) if part < STEPS - 1 else (end + GROUP * WIDE - 1) // (GROUP * WIDE)
        lax.fori_loop(done, end, step, 0)
        done = end
    for refs, owner_core in ((away_refs, 1 - core), (home_refs, core)):
        for shift, ref in enumerate(refs):
            first = pl.multiple_of(owner_core * SPOTS + shift * OWN_DEV, OWN_DEV)
            ref[...] = total[pl.ds(first, OWN_DEV)].astype(ref.dtype)


def products(me, listed, lefts, rights):
    shape = (OWN_DEV, QUARTER, TILE)
    types = [BF16] * N_X + [F32] + [BF16] * (N_X - 1)
    return pl.pallas_call(
        products_kernel,
        out_shape=[jax.ShapeDtypeStruct(shape, kind) for kind in types],
        in_specs=[SMEM] * 2 + [ANY] * (N_SRC + N_RIGHT),
        out_specs=[VMEM] * (2 * N_X),
        scratch_shapes=[
            pltpu.VMEM((N_SRC, ROWS, TILE), BF16),
            pltpu.VMEM((N_REP, NB, QUARTER, TILE), BF16),
            pltpu.VMEM((2 * SPOTS + 1, QUARTER, TILE), F32),
            pltpu.SemaphoreType.DMA((N_SRC,)),
            pltpu.SemaphoreType.DMA((N_REP * STEPS,)),
        ],
        compiler_params=pltpu.CompilerParams(vmem_limit_bytes=VMEM_LIMIT),
        cost_estimate=pl.CostEstimate(
            flops=2 * 384 * 64 * 256 * 256, bytes_accessed=10 << 20, transcendentals=0
        ),
        name="products",
    )(me, listed, *lefts, *rights)


def shift_by(value, axis, size, step):
    return lax.ppermute(value, axis, [(i, (i + step) % size) for i in range(size)])


def apart(value, axis, size):
    perm = []
    for i in range(size):
        perm.append((i * 2, ((i + 1) % size) * 2))
        perm.append((i * 2 + 1, ((i - 1) % size) * 2 + 1))
    return lax.ppermute(value, (axis, "core"), perm)


def other_core(value):
    return lax.ppermute(value, "core", [(0, 1), (1, 0)])


def gather(mine, half):
    back = shift_by(half, "rep", N_REP, 1)
    ahead = shift_by(half, "rep", N_REP, -1)
    own, other = mine, other_core(mine)
    blocks = [own]
    for distance in range(3):
        own, other = apart(own, "z", N_Z), apart(other, "z", N_Z)
        blocks += [own, other]
        if distance == 1:
            back, ahead, _ = lax.optimization_barrier((back, ahead, other))
    far_back = shift_by(back[: HALF // 2], "rep", N_REP, 1)
    far_ahead = shift_by(ahead[HALF // 2 :], "rep", N_REP, -1)
    parts = [back, far_back, far_ahead, ahead]
    return blocks + [apart(own, "z", N_Z)], parts + [other_core(part) for part in parts]


def body(amps, integrals, a_index, b_index, live, owner, target):
    rep, z, x, core = [lax.axis_index(n).astype(I32) for n in ("rep", "z", "x", "core")]
    x, *pieces = lax.optimization_barrier((x, *spread_rows(rep[None], amps)))
    half = lax.dynamic_slice_in_dim(integrals, core * HALF, HALF, 0)
    table = product_table(x[None], a_index, b_index, live, owner, target)
    parts = [pieces[0]] + [shift_by(pieces[s], "rep", N_REP, s) for s in range(1, N_REP)]
    half, table = lax.optimization_barrier((half, table))
    lefts, rights = gather(join_k(table, parts), half)
    me = jnp.stack([z, core])
    sums = products(me, sort_products(me, lefts), lefts, [integrals] + rights)
    total = None
    for shift in (2, 1, 3, 0):
        part = sums[N_X + shift].astype(F32) + other_core(sums[shift]).astype(F32)
        if shift > 0:
            part = shift_by(part.astype(BF16), "x", N_X, shift).astype(F32)
        total = part if total is None else total + part
    return total


def solution(mesh):
    devices = mesh.devices.reshape(N_REP, N_Z, N_X, N_CORE)
    fine = Mesh(devices, ("rep", "z", "x", "core"))
    task = ("z", "x", "core")
    in_specs = (
        P(task, None, "rep"),
        P(None, "rep", None),
        P(task),
        P(task),
        P(task),
        P(task, None),
        P(task),
    )
    return jax.shard_map(
        body, mesh=fine, in_specs=in_specs, out_specs=P(task, "rep", None), check_vma=False
    )
```
